1024 devices in a mesh: wave: 128 (over y, z), ocean: 8 (over x, core).
Axes of the slice: x: 4, y: 8, z: 16, core: 2. Of those that a mesh axis runs over, the one named last changes fastest.
Arguments:
- spectra: float32 [128, 36, 36, 1024], P('wave', None, None, 'ocean'), may hold values from 0.2 to 2, as said below
- surface_wind: float32 [2, 128, 1024], P(None, 'wave', 'ocean'), may hold values from -6.5 to 6.5
- water_mask: int32 [128, 1024], P('wave', 'ocean'), may hold values 0 or 1
- send_rows: int32 [8, 65536], P(None, ('wave', 'ocean')), may hold values from 0 to 127, as said below
- send_count: int32 [8, 1024], P(None, ('wave', 'ocean')), may hold values from 8 to 64, as said below
- pick_slot: int32 [4, 524288], P(None, ('wave', 'ocean')), may hold values from 0 to 511, as said below
- pick_weight: float32 [4, 524288], P(None, ('wave', 'ocean')), may hold values from 0.05 to 0.5
- ocean_current: float32 [2, 524288], P(None, ('wave', 'ocean')), may hold values from -4 to 4
Outputs:
- ocean_forcing: float32 [34, 524288], P(None, ('wave', 'ocean'))
- wave_current: float32 [2, 128, 1024], P(None, 'wave', 'ocean')
The draws below stay inside these ranges and needn't reach their ends.
Inputs may be any that keep to these rules, and one draw needn't show every extreme that they name: `spectra`: energy density of each spectral bin. `send_rows`: indices of the sending device's own wave points, numbered row-major over its 1 x 128 block. `send_count`: in every strip one owner receives 64 live rows from every device of the strip. `pick_slot`: source owner times 64 plus a slot below that source's live count toward this device.
All inputs are finite; a program needn't handle non-finite values. No bound on the sum of `water_mask` on one device may be relied on, other than what follows from the above.
Results may differ from the reference program's by a relative error of at most 0.0003.
Values sent between devices are 32-bit elements; how exact they have to be, the bound alone decides.
A program may use at most 32 MiB of HBM per device.

```python
import math
from functools import partial
import jax
import jax.numpy as jnp
from jax import lax

GX = 1
GY = 128
ND = 36
NF = 36
DEPTHS = 16
KNB = 4
CH = 34
CAP = 64
OPTS = 512
STRIPS = 128
OWNERS = 8
NXW = 128
NYW = 1024
N_WAVE = 128
N_OCEAN = 8


def regrid_counts(key):
    base_key = jax.random.fold_in(key, 7)
    first_key, second_key = jax.random.split(base_key)
    base_load = jax.random.randint(first_key, (STRIPS, OWNERS, OWNERS), max(CAP // 8, 1), CAP // 2 + 1)
    busiest = jax.random.randint(second_key, (STRIPS,), 0, OWNERS)
    owner_ids = jnp.arange(OWNERS, dtype=jnp.int32)
    is_full = owner_ids[None, None, :] == busiest[:, None, None]
    return (jnp.where(is_full, CAP, base_load).astype(jnp.int32), busiest)


def draw_send_count(key, part):
    counts, busiest = regrid_counts(key)
    return counts.transpose(2, 0, 1).reshape(OWNERS, STRIPS * OWNERS).astype(jnp.int32)


def draw_send_rows(key, part):
    key = jax.random.fold_in(key, 21)
    row_ids = jax.random.randint(key, (OWNERS, STRIPS * OWNERS * CAP), 0, GX * GY)
    return row_ids.at[0, 0].set(GX * GY - 1).astype(jnp.int32)


def draw_pick_slot(key, part):
    counts, busiest = regrid_counts(key)
    key = jax.random.fold_in(key, 33)
    source_key, slot_key = jax.random.split(key)
    source = jax.random.randint(source_key, (STRIPS, OWNERS, KNB, OPTS), 0, OWNERS)
    strip_ids = jnp.arange(STRIPS, dtype=jnp.int32)[:, None, None, None]
    owner_ids = jnp.arange(OWNERS, dtype=jnp.int32)[None, :, None, None]
    limits = counts[strip_ids, source, owner_ids]
    slot_ids = jax.random.randint(slot_key, (STRIPS, OWNERS, KNB, OPTS), 0, limits)
    picked = source * CAP + slot_ids
    picked = picked.at[jnp.arange(STRIPS), busiest, 0, 0].set(OWNERS * CAP - 1)
    return picked.transpose(2, 0, 1, 3).reshape(KNB, STRIPS * OWNERS * OPTS).astype(jnp.int32)


def draw_spectra(key, part):
    key = jax.random.fold_in(key, 41)
    mode_key, other_key, phase_key, second_key, rough_key = jax.random.split(key, 5)
    first_mode = jax.random.randint(mode_key, (NXW, 1, 1, NYW), 3, 7).astype(jnp.float32)
    second_mode = jax.random.randint(other_key, (NXW, 1, 1, NYW), 8, 14).astype(jnp.float32)
    first_phase = jax.random.uniform(phase_key, (NXW, 1, 1, NYW), jnp.float32, 0.0, 2.0 * jnp.pi)
    second_phase = jax.random.uniform(second_key, (NXW, 1, 1, NYW), jnp.float32, 0.0, 2.0 * jnp.pi)
    angles = ((jnp.arange(ND, dtype=jnp.float32) + 0.5) * (2.0 * jnp.pi / ND)).reshape(1, ND, 1, 1)
    first_weight = 0.35
    second_weight = 0.4
    roughness = jnp.exp(jax.random.uniform(rough_key, (NXW, ND, NF, NYW), jnp.float32, jnp.log(0.8), jnp.log(1.14)))
    pattern = 1.0 + first_weight * jnp.cos(first_mode * angles + first_phase) + second_weight * jnp.cos(second_mode * angles + second_phase)
    return (roughness * pattern).astype(jnp.float32)


def draw_surface_wind(key, part):
    key = jax.random.fold_in(key, 53)
    heading_key, jitter_key, wind_key = jax.random.split(key, 3)
    heading = jax.random.uniform(heading_key, (NXW, 1), jnp.float32, -jnp.pi, jnp.pi)
    jitter = jax.random.uniform(jitter_key, (NXW, NYW), jnp.float32, -0.8, 0.8)
    wind_speed = jnp.exp(jax.random.uniform(wind_key, (NXW, NYW), jnp.float32, jnp.log(3.0), jnp.log(6.5)))
    wind_angle = heading + jitter
    return jnp.stack([wind_speed * jnp.cos(wind_angle), wind_speed * jnp.sin(wind_angle)], 0).astype(jnp.float32)


def set_ends(drawn, own_key, low, largest):
    longest = drawn.shape.index(max(drawn.shape))
    spots = []
    for shift in (0, 1):
        where = [jax.random.randint(jax.random.fold_in(own_key, axis), (), 0, length) for axis, length in enumerate(drawn.shape)]
        where[longest] = (where[longest] + shift) % drawn.shape[longest]
        spots.append(tuple(where))
    return drawn.at[spots[0]].set(low).at[spots[1]].set(largest)


def shard_levels(stream_key, dims, cuts, low, largest):
    loudness = 1.0
    for position, blocks in cuts:
        steps = jax.random.uniform(jax.random.fold_in(jax.random.fold_in(stream_key, 6), position), (blocks,), jnp.float32, low / len(cuts), largest / len(cuts))
        loudness = loudness * jnp.repeat(jnp.exp(steps), dims[position] // blocks).reshape((-1,) + (1,) * (len(dims) - 1 - position))
    return loudness


def scatter_about(own_key, extent, spread, most, cuts=(), kind=jnp.bfloat16):
    array = spread * jax.random.normal(own_key, extent, jnp.float32)
    if cuts:
        array = array * shard_levels(own_key, extent, cuts, -0.22, 0.18)
    return jnp.clip(array, -most, most).astype(kind)


def setup_inputs(seed: int = 0) -> dict:
    key_of = jax.random.split(jax.random.key(seed), 9)
    return {
        "spectra": draw_spectra(jax.random.fold_in(key_of[8], 71), 0),
        "surface_wind": draw_surface_wind(jax.random.fold_in(key_of[8], 71), 0),
        "water_mask": set_ends((jax.random.randint(key_of[2], (NXW, NYW), 0, 10) < 7).astype(jnp.int32), jax.random.fold_in(key_of[2], 1), 0, 1),
        "send_rows": draw_send_rows(jax.random.fold_in(key_of[8], 71), 0),
        "send_count": draw_send_count(jax.random.fold_in(key_of[8], 71), 0),
        "pick_slot": draw_pick_slot(jax.random.fold_in(key_of[8], 71), 0),
        "pick_weight": jnp.clip(jnp.exp(math.log(0.5) - 2.3025851 * jax.random.uniform(key_of[6], (KNB, OPTS * N_WAVE * N_OCEAN), jnp.float32) ** shard_levels(key_of[6], (KNB, OPTS * N_WAVE * N_OCEAN), ((1, 1024),), -0.2, 0.2)), 0.05, 0.5),
        "ocean_current": scatter_about(key_of[7], (2, OPTS * N_WAVE * N_OCEAN), 0.5, 4.0, ((1, 1024),), jnp.float32),
    }


def tables():
    headings = jnp.arange(ND, dtype=jnp.float32)
    angles = (headings + 0.5) * (2.0 * jnp.pi / ND)
    cosine = jnp.cos(angles)
    sines = jnp.sin(angles)
    frequency = jnp.arange(NF, dtype=jnp.float32)
    speeds = 0.7 * jnp.power(1.1, -frequency)
    ratios = jnp.power(1.1, frequency - (NF - 1))
    kappas = 0.02 * jnp.power(1.1, 2.0 * frequency)
    depths = 0.25 * jnp.arange(DEPTHS, dtype=jnp.float32)
    kernel = jnp.sqrt(kappas)[:, None] * jnp.exp(-2.0 * kappas[:, None] * depths[None, :])
    return (cosine, sines, speeds, ratios, kernel)

def driving(surface_wind, cosine, sines):
    return jax.nn.relu(surface_wind[0][:, None, None, :] * cosine[None, :, None, None] + surface_wind[1][:, None, None, :] * sines[None, :, None, None])

def advance(padded, surface_wind, ocean_cells, cosine, sines, speeds, ratios):
    centre = padded[1:-1, :, :, 1:-1]
    behind_x = padded[:-2, :, :, 1:-1]
    ahead_x = padded[2:, :, :, 1:-1]
    behind_y = padded[1:-1, :, :, :-2]
    ahead_y = padded[1:-1, :, :, 2:]
    along_x = (cosine[:, None] * speeds[None, :])[None, :, :, None]
    along_y = (sines[:, None] * speeds[None, :])[None, :, :, None]
    advected = centre - jnp.maximum(along_x, 0.0) * (centre - behind_x) - jnp.minimum(along_x, 0.0) * (ahead_x - centre) - jnp.maximum(along_y, 0.0) * (centre - behind_y) - jnp.minimum(along_y, 0.0) * (ahead_y - centre)
    energy = lax.optimization_barrier(jnp.mean(advected, axis=(1, 2), keepdims=True))
    rates = ratios[None, None, :, None]
    factor = 1.0 + 0.1 * rates * driving(surface_wind, cosine, sines) - 0.3 * rates * energy / (energy + 1.0)
    return ocean_cells[:, None, None, :] * advected * factor

def project(spectrum, surface_wind, cosine, sines, ratios, kernel):
    weights_s = jnp.concatenate([cosine[:, None, None] * kernel[None], sines[:, None, None] * kernel[None]], 2) / ND
    stokes = jnp.einsum('xdfy,dfc->cxy', spectrum, weights_s, precision=lax.Precision.HIGHEST)
    pushed = spectrum * (0.1 * ratios[None, None, :, None]) * driving(surface_wind, cosine, sines)
    compass = jnp.stack([cosine, sines], 1) / ND
    stress = jnp.einsum('xdfy,dc->cxy', pushed, compass, precision=lax.Precision.HIGHEST)
    return jnp.concatenate([stokes, stress], 0)

def pack_rows(column_collection, row_ids, number_of_rows):
    owners, slot_grand_sum = row_ids.shape
    active_flag = (jnp.arange(slot_grand_sum, dtype=jnp.int32)[None, :] < number_of_rows[:, None]).astype(jnp.float32)
    collected_values = jnp.take(column_collection, row_ids.reshape(-1), axis=1).reshape(column_collection.shape[0], owners, slot_grand_sum)
    return collected_values * active_flag[None]

def blend_slots(received, picked, weights):
    values = jnp.take(received, picked.reshape(-1), axis=1).reshape(received.shape[0], picked.shape[0], picked.shape[1])
    return lax.optimization_barrier(jnp.sum(values * weights[None], axis=1))

def spread_values(current, picked, weights, slot_grand_sum):
    carried = jnp.concatenate([current, jnp.ones((1, current.shape[1]), jnp.float32)], 0)
    weighted = (carried[:, None, :] * weights[None]).reshape(3, -1)
    return jnp.zeros((3, slot_grand_sum), jnp.float32).at[:, picked.reshape(-1)].add(weighted)

def settle(returned, row_ids, points):
    totals = jnp.zeros((3, points), jnp.float32).at[:, row_ids.reshape(-1)].add(returned.reshape(3, -1))
    return totals[:2] / jnp.maximum(totals[2:], 1.0)

def reference(spectra, surface_wind, water_mask, send_rows, send_count, pick_slot, pick_weight, ocean_current):
    cosine, sines, speeds, ratios, kernel = tables()
    ocean_cells = water_mask.astype(jnp.float32)
    strips = jnp.arange(N_WAVE, dtype=jnp.int32)
    flanks = ((1, 1), (0, 0), (0, 0), (1, 1))
    padded_first = jnp.pad(spectra, flanks)

    def first_strip(strip):
        offset = strip * GX
        window = lax.dynamic_slice_in_dim(padded_first, offset, GX + 2, 0)
        wind_here = lax.dynamic_slice_in_dim(surface_wind, offset, GX, 1)
        mask_here = lax.dynamic_slice_in_dim(ocean_cells, offset, GX, 0)
        return advance(window, wind_here, mask_here, cosine, sines, speeds, ratios)
    after_one = lax.map(first_strip, strips).reshape(NXW, ND, NF, NYW)
    padded_second = jnp.pad(after_one, flanks)

    def second_strip(strip):
        offset = strip * GX
        window = lax.dynamic_slice_in_dim(padded_second, offset, GX + 2, 0)
        wind_here = lax.dynamic_slice_in_dim(surface_wind, offset, GX, 1)
        mask_here = lax.dynamic_slice_in_dim(ocean_cells, offset, GX, 0)
        after_second_step = advance(window, wind_here, mask_here, cosine, sines, speeds, ratios)
        return project(after_second_step, wind_here, cosine, sines, ratios, kernel)
    fields = lax.map(second_strip, strips)
    tiles = fields.reshape(N_WAVE, CH, GX, N_OCEAN, GY).transpose(0, 3, 1, 2, 4).reshape(N_WAVE, N_OCEAN, CH, GX * GY)
    row_ids = send_rows.reshape(N_OCEAN, N_WAVE, N_OCEAN, CAP).transpose(1, 2, 0, 3)
    counts = send_count.reshape(N_OCEAN, N_WAVE, N_OCEAN).transpose(1, 2, 0)
    packed = jax.vmap(jax.vmap(pack_rows))(tiles, row_ids, counts)
    received = packed.transpose(0, 3, 2, 1, 4).reshape(N_WAVE, N_OCEAN, CH, N_OCEAN * CAP)
    picks = pick_slot.reshape(KNB, N_WAVE, N_OCEAN, OPTS).transpose(1, 2, 0, 3)
    weights = pick_weight.reshape(KNB, N_WAVE, N_OCEAN, OPTS).transpose(1, 2, 0, 3)
    forcing = jax.vmap(jax.vmap(blend_slots))(received, picks, weights)
    ocean_forcing = forcing.transpose(2, 0, 1, 3).reshape(CH, N_WAVE * N_OCEAN * OPTS)
    currents = ocean_current.reshape(2, N_WAVE, N_OCEAN, OPTS).transpose(1, 2, 0, 3)
    slot_sums = jax.vmap(jax.vmap(partial(spread_values, slot_grand_sum=N_OCEAN * CAP)))(currents, picks, weights)
    returned = slot_sums.reshape(N_WAVE, N_OCEAN, 3, N_OCEAN, CAP).transpose(0, 3, 2, 1, 4)
    wave_parts = jax.vmap(jax.vmap(partial(settle, points=GX * GY)))(returned, row_ids)
    wave_current = wave_parts.reshape(N_WAVE, N_OCEAN, 2, GX, GY).transpose(2, 0, 3, 1, 4).reshape(2, NXW, NYW)
    return (ocean_forcing, wave_current)
```

```python
import functools

import jax
import jax.numpy as jnp
import ml_dtypes
import numpy as np
from jax import lax
from jax.experimental import pallas as pl
from jax.experimental.pallas import tpu as pltpu
from jax.sharding import PartitionSpec as P

ND = 36
NF = 36
FP = 40
DEPTHS = 16
CAP = 64
QUAD = 9
MESH = pl.DeviceIdType.MESH
F32 = jnp.float32
BF16 = jnp.bfloat16
HALVES = ((0, 16), (16, 20))
EDGE = QUAD * 2 * NF


def host_tables():
    angles = (np.arange(ND) + 0.5) * (2.0 * np.pi / ND)
    cosine, sines = np.cos(angles), np.sin(angles)
    frequency = np.arange(NF)
    speeds = 0.7 * 1.1 ** (-frequency)
    ratios = 1.1 ** (frequency - (NF - 1.0))
    kappas = 0.02 * 1.1 ** (2.0 * frequency)
    depths = 0.25 * np.arange(DEPTHS)
    kernel = np.sqrt(kappas)[:, None] * np.exp(-2.0 * kappas[:, None] * depths[None, :])
    return cosine, sines, speeds, ratios, kernel


def split_rows(values):
    high = values.astype(ml_dtypes.bfloat16)
    low = (values - high.astype(np.float64)).astype(ml_dtypes.bfloat16)
    return np.concatenate([high, low], 0).astype(np.float32)


def projection(scale):
    _, _, _, ratios, kernel = host_tables()
    table = np.zeros((80, 256))

    def put(row, group, values):
        table[row, group * FP : group * FP + NF] = values * scale / ND

    for depth in range(DEPTHS):
        k = kernel[:, depth]
        for side in (0, 1):
            put(16 * side + depth, side, k)
            put(16 * side + depth, 2 + side, k * ratios)
            put(40 + 16 * side + depth, side, 0.3 * k * ratios)
    for side in (0, 1):
        put(32 + side, 4 + side, ratios)
        put(72 + side, 2 + side, 0.3 * ratios * ratios)
    return split_rows(table)


def constants():
    cosine, sines, speeds, ratios, _ = host_tables()
    ac, an = np.abs(cosine), np.abs(sines)
    coef = np.zeros((ND, 16))
    for i, column in enumerate((ac, an, cosine * ac, sines * ac, cosine * an, sines * an, cosine, sines, ac + an)):
        coef[:, i] = column
    wide = np.zeros((4, FP, 128))
    for i, column in enumerate((speeds, ratios, cosine, sines)):
        wide[i, :36] = column[:, None]
    return (
        coef.astype(np.float32),
        wide.astype(np.float32),
        projection(np.ones(NF)),
        projection(speeds),
    )


def mxu(a, b, dims=(((1,), (0,)), ((), ()))):
    return lax.dot_general(a, b, dims, preferred_element_type=F32)


def split(x):
    high = x.astype(BF16)
    return high, (x - high.astype(F32)).astype(BF16)


def interval(
    strips,
    owners,
    opts,
    coef,
    spectra,
    flat,
    wind_hbm,
    mask_hbm,
    rows_hbm,
    count_hbm,
    pick_hbm,
    weight_hbm,
    current_hbm,
    wide_hbm,
    wown_hbm,
    wxy_hbm,
    forcing,
    back,
    e_v,
    ex_v,
    m_v,
    flat_v,
    edge_v,
    wind,
    mask,
    rows,
    count,
    pick,
    weight,
    current,
    wide,
    wown,
    wxy,
    drive,
    sx_v,
    xq,
    yq,
    oq,
    eq,
    xs,
    xr,
    ys,
    yr,
    ps,
    pr,
    rs,
    rr,
    fs,
    fr,
    ts,
    tr,
    m2,
    b2,
    car,
    local_sem,
    send_sem,
    recv_sem,
):
    w, o = lax.axis_index("wave"), lax.axis_index("ocean")
    xp, xm = (lax.rem(w + 1, strips), o), (lax.rem(w + strips - 1, strips), o)
    yp, ym = (w, lax.rem(o + 1, owners)), (w, lax.rem(o + owners - 1, owners))

    def peer(j):
        return (w, lax.rem(o + j, owners))

    barrier = pltpu.get_barrier_semaphore()
    for device in (xp, xm, *(peer(j) for j in range(1, owners))):
        pl.semaphore_signal(barrier, inc=1, device_id=device, device_id_type=MESH)

    loads = []
    for src, dst in (
        (spectra.at[:, :, 0, :], e_v),
        (wind_hbm, wind),
        (wide_hbm, wide),
        (flat, flat_v),
        (rows_hbm, rows),
        (count_hbm, count),
        (mask_hbm, mask),
        (pick_hbm, pick),
        (weight_hbm, weight),
        (current_hbm, current),
        (wxy_hbm, wxy),
        (wown_hbm, wown),
    ):
        cp = pltpu.make_async_copy(src, dst, local_sem.at[len(loads)])
        cp.start()
        loads.append(cp)

    used = [0]

    def send(src, dst, device):
        i = used[0]
        used[0] += 1
        cp = pltpu.make_async_remote_copy(
            src_ref=src, dst_ref=dst, send_sem=send_sem.at[i], recv_sem=recv_sem.at[i], device_id=device, device_id_type=MESH
        )
        cp.start()
        return cp

    left_in = jnp.where(w > 0, 1.0, 0.0).astype(F32)
    right_in = jnp.where(w < strips - 1, 1.0, 0.0).astype(F32)
    down_in = jnp.where(o > 0, 1.0, 0.0).astype(F32)
    up_in = jnp.where(o < owners - 1, 1.0, 0.0).astype(F32)
    lane = lax.broadcasted_iota(jnp.int32, (1, 128), 1)

    for ref in (xq, yq, oq):
        ref[...] = jnp.zeros(ref.shape, F32)
    eq[...] = jnp.zeros(eq.shape, F32)

    for cp in loads[:3]:
        cp.wait()
    s_all, r_all = wide[0, 0:NF, :], wide[1, 0:NF, :]
    sums = []
    for q in range(4):

        def gather_energy(i, acc, q=q):
            d = q * QUAD + i
            e = e_v[d]
            return acc[0] + e, acc[1] + coef[d, 0] * e, acc[2] + coef[d, 1] * e

        zero = jnp.zeros((NF, 128), F32)
        sums.append(lax.fori_loop(0, QUAD, gather_energy, (zero, zero, zero), unroll=3))

    def over_f(x):
        return jnp.sum(x, axis=0, keepdims=True)

    gc = [x[1] for x in sums]
    gn = [x[2] for x in sums]
    en_xp, en_xm = over_f(s_all * (gc[0] + gc[3])), over_f(s_all * (gc[1] + gc[2]))
    en_yp, en_ym = over_f(s_all * (gn[0] + gn[1])), over_f(s_all * (gn[2] + gn[3]))
    en_own = over_f(sums[0][0] + sums[1][0] + sums[2][0] + sums[3][0]) - (en_xp + en_xm + en_yp + en_ym)
    en_yp, en_ym = pltpu.roll(en_yp, 1, 1), pltpu.roll(en_ym, 127, 1)

    w0, w1 = wind[0], wind[1]
    row8 = lax.broadcasted_iota(jnp.int32, (8, 128), 0)

    def tile(energy):
        return jnp.where(row8 == 0, energy, jnp.where(row8 == 1, w0, w1))

    xs[0], xs[1] = tile(en_xp), tile(en_xm)

    pl.semaphore_wait(barrier, owners + 1)
    early_x = [send(xs.at[0], xr.at[0], xp), send(xs.at[1], xr.at[1], xm)]
    chunk = {}
    for q in (0, 2, 3, 1):
        part = pl.ds(q * QUAD, QUAD)
        chunk[q] = send(spectra.at[part, :, 0, :], ex_v.at[part], xp if q in (0, 3) else xm)

    for cp in loads[3:]:
        cp.wait()
    for side, last in ((0, 127), (1, 0)):
        pickup = jnp.where(lax.broadcasted_iota(jnp.int32, (16, 128), 1) == last, 1.0, 0.0).astype(BF16)
        high, low = split(flat_v[pl.ds(side * EDGE, EDGE), :])
        turned = (((1,), (1,)), ((), ()))
        ys[side, :, 0:128] = tile(en_yp if side == 0 else en_ym)
        ys[side, :, 128 : 128 + EDGE] = (mxu(pickup, high, turned) + mxu(pickup, low, turned))[0:8]
        ys[side, :, 128 + EDGE : 896] = jnp.zeros((8, 768 - EDGE), F32)
    early_y = [send(ys.at[0], yr.at[0], yp), send(ys.at[1], yr.at[1], ym)]

    lane8 = lax.broadcasted_iota(jnp.int32, (1, owners), 1)
    for j in range(owners):
        to = lax.rem(o + j, owners)
        picked = rows[pl.ds(to, 1), :]
        live = jnp.sum(jnp.where(lane8 == to, count[...], 0).astype(F32), axis=1, keepdims=True).astype(jnp.int32)
        both = jnp.concatenate([picked, picked], axis=1)
        rs[j] = jnp.where(row8 == 0, both, jnp.broadcast_to(live, (8, 128)))
    lists = {j: send(rs.at[j], rr.at[j], peer(j)) for j in range(1, owners)}
    rr[0] = rs[0]

    for j in range(owners):
        source = lax.rem(o + owners - j, owners)
        slots = lax.broadcasted_iota(jnp.int32, (CAP, opts), 0) + source * CAP
        total = jnp.zeros((CAP, opts), F32)
        for k in range(4):
            total = total + jnp.where(pick[k : k + 1, :] == slots, weight[k : k + 1, :], 0.0)
        high, low = split(total)
        m2[j, 0:CAP, :] = high
        m2[j, CAP : 2 * CAP, :] = low

    for cp in early_x + early_y:
        cp.wait_recv()
    ct, nt = wide[2, 0:NF, :], wide[3, 0:NF, :]

    def driving(a, b):
        return 0.1 * jnp.maximum(a * ct + b * nt, 0.0)

    drive[0] = driving(w0, w1)
    drive[1] = jnp.where(
        ct > 0, driving(xr[1, 1:2, :], xr[1, 2:3, :]), driving(xr[0, 1:2, :], xr[0, 2:3, :])
    )
    up0 = jnp.where(lane == 127, pltpu.roll(yr[1, 1:2, 0:128], 127, 1), pltpu.roll(w0, 127, 1))
    up1 = jnp.where(lane == 127, pltpu.roll(yr[1, 2:3, 0:128], 127, 1), pltpu.roll(w1, 127, 1))
    dn0 = jnp.where(lane == 0, pltpu.roll(yr[0, 1:2, 0:128], 1, 1), pltpu.roll(w0, 1, 1))
    dn1 = jnp.where(lane == 0, pltpu.roll(yr[0, 2:3, 0:128], 1, 1), pltpu.roll(w1, 1, 1))
    drive[2] = jnp.where(nt > 0, driving(up0, up1), driving(dn0, dn1))
    energy = (
        en_own
        + left_in * xr[0, 0:1, :]
        + right_in * xr[1, 0:1, :]
        + jnp.where(lane == 0, down_in * yr[0, 0:1, 0:128], en_yp)
        + jnp.where(lane == 127, up_in * yr[1, 0:1, 0:128], en_ym)
    ) * (1.0 / (ND * NF))
    damp = 0.3 * (energy / (energy + 1.0))
    sx_v[0] = s_all * left_in
    sx_v[1] = s_all * right_in

    for side, (last, inside, shift) in enumerate(((0, down_in, 1), (127, up_in, 127))):
        place = jnp.where(lax.broadcasted_iota(jnp.int32, (16, 128), 1) == last, 1.0, 0.0)
        place = jnp.where(lax.rem(lax.broadcasted_iota(jnp.int32, (16, 128), 0), 8) == 0, place, 0.0).astype(BF16)
        high, low = split(yr[side, :, 128 : 128 + EDGE] * inside)
        both = jnp.concatenate([high.astype(F32), low.astype(F32)], axis=0).astype(BF16)
        edge_v[side] = mxu(both, place, (((0,), (0,)), ((), ())))
        for half in (0, 1):
            for i in range(QUAD):
                d = side * 2 * QUAD + half * QUAD + i
                e = e_v[d]
                k = (half * QUAD + i) * NF
                behind = jnp.where(lane == last, edge_v[side, k : k + NF, :], pltpu.roll(e, shift, 1))
                m_v[d] = e + s_all * (coef[d, 1] * behind - coef[d, 8] * e)

    carried = current[...]
    ones = jnp.ones((1, opts), F32)
    c_high = carried.astype(BF16).astype(F32)
    none = jnp.zeros((5, opts), F32)
    car[...] = jnp.concatenate([c_high, ones, none, carried - c_high, jnp.zeros((6, opts), F32)], axis=0).astype(BF16)
    point = lax.broadcasted_iota(jnp.int32, (128, 128), 0)
    slot = lax.rem(lax.broadcasted_iota(jnp.int32, (1, 128), 1), CAP)
    for j in range(owners):
        if j:
            lists[j].wait_recv()
        hit = jnp.logical_and(rr[j, 0:1, :] == point, slot < rr[j, 1:2, :])
        matrix = mxu(jnp.where(hit, 1.0, 0.0).astype(BF16), m2[j])
        high, low = split(matrix)
        b2[j, 0:128, :] = high
        b2[j, 128:256, :] = low
        t = mxu(car[...], b2[j], (((1,), (1,)), ((), ())))
        ts[j] = t[0:8, 0:128] + t[8:16, 0:128] + t[0:8, 128:256] + t[8:16, 128:256]
    returns = {j: send(ts.at[j], tr.at[j], peer(owners - j)) for j in range(1, owners)}

    seen = set()
    for q in (0, 2, 3, 1):
        chunk[q].wait_recv()
        x_side, y_side = (0 if q in (0, 3) else 1), (0 if q in (0, 1) else 1)
        for low, n in HALVES:
            part = pl.ds(low, n)
            r = wide[1, part, :]
            sx = sx_v[x_side, part, :]

            def bins(i, acc, q=q, part=part, r=r, sx=sx):
                d = q * QUAD + i
                moved = m_v[d, part, :] + sx * (coef[d, 0] * ex_v[d, part, :])
                e = moved + moved * (r * (drive[0, pl.ds(d, 1), :] - damp))
                m_v[d, part, :] = e
                out = []
                for at, (a, kc, kn) in ((1, (0, 2, 3)), (2, (1, 4, 5))):
                    here = drive[at, pl.ds(d, 1), :]
                    e1 = e * here
                    e2 = e1 * here
                    a, kc, kn = coef[d, a], coef[d, kc], coef[d, kn]
                    out += [a * e, kc * e, kn * e, kc * e1, kn * e1, kc * e2, kn * e2]
                return tuple(x + y for x, y in zip(acc, out))

            acc = lax.fori_loop(0, QUAD, bins, (jnp.zeros((n, 128), F32),) * 14, unroll=3)
            for ref, side, kind, a in ((xq, x_side, 0, acc[:7]), (yq, y_side, 1, acc[7:])):
                col = pl.ds(side * 128, 128)
                parts = [a[1], a[2], a[3], a[4], a[3] + r * a[5], a[4] + r * a[6]]
                again = (kind, side, low) in seen
                seen.add((kind, side, low))
                for g, value in enumerate(parts):
                    at = pl.ds(g * FP + low, n)
                    ref[at, col] = ref[at, col] + value if again else value
                at = pl.ds(low, n)
                eq[2 * kind + side, at, :] = eq[2 * kind + side, at, :] + a[0] if again else a[0]

    sea = mask[...].astype(F32)

    def contract(table, x):
        high, low = split(x)
        both = table[...].astype(BF16)
        out = mxu(both, high)
        return out[0:80] + out[80:160] + mxu(both[0:80], low)

    def finish(value, energy_row):
        tail = value[32:40] + jnp.where(row8 == 2, energy_row, 0.0)
        return sea * jnp.concatenate([value[0:32], tail, value[40:80]], axis=0)

    s_pad = wide[0]
    out = contract(wxy, xq[...])
    for side in (0, 1):
        ps[side] = finish(out[:, side * 128 : side * 128 + 128], over_f(s_pad * eq[side]))
    sums_out = [send(ps.at[0], pr.at[0], xp), send(ps.at[1], pr.at[1], xm)]
    out = contract(wxy, yq[...])
    for side in (0, 1):
        value = finish(out[:, side * 128 : side * 128 + 128], over_f(s_pad * eq[2 + side]))
        ps[2 + side] = pltpu.roll(value, (1, 127)[side], 1)
    sums_out += [send(ps.at[2], pr.at[2], yp), send(ps.at[3], pr.at[3], ym)]

    e_own = []
    for low, n in HALVES:
        part = pl.ds(low, n)
        r, s = wide[1, part, :], wide[0, part, :]

        def own_bins(d, acc, part=part, s=s):
            e = m_v[d, part, :]
            e = e - s * (coef[d, 8] * e)
            here = drive[0, pl.ds(d, 1), :]
            e1 = e * here
            e2 = e1 * here
            kc, kn = coef[d, 6], coef[d, 7]
            out = (e, kc * e, kn * e, kc * e1, kn * e1, kc * e2, kn * e2)
            return tuple(x + y for x, y in zip(acc, out))

        a = lax.fori_loop(0, ND, own_bins, (jnp.zeros((n, 128), F32),) * 7, unroll=4)
        for g, value in enumerate([a[1], a[2], a[3], a[4], a[3] + r * a[5], a[4] + r * a[6]]):
            oq[pl.ds(g * FP + low, n), :] = value
        e_own.append(over_f(a[0]))
    total = finish(contract(wown, oq[...]), e_own[0] + e_own[1])

    for j in range(1, owners):
        returns[j].wait_recv()
    got = ts[0]
    for j in range(1, owners):
        got = got + tr[j]
    back[:, 0, :] = got[0:2] / jnp.maximum(got[2:3], 1.0)

    for cp in sums_out:
        cp.wait_recv()
    total = (
        total
        + left_in * pr[0]
        + right_in * pr[1]
        + jnp.where(lane == 0, down_in * pr[2], ps[2])
        + jnp.where(lane == 127, up_in * pr[3], ps[3])
    )
    energy = total[34:35] * (1.0 / (ND * NF))
    fs[...] = sea * (total[0:40] - (energy / (energy + 1.0)) * total[40:80])
    fields = {j: send(fs, fr.at[j], peer(j)) for j in range(1, owners)}

    acc = jnp.zeros((80, opts), F32)
    for j in range(owners):
        if j:
            fields[j].wait_recv()
        value = fr[j] if j else fs[...]
        high = value.astype(BF16).astype(F32)
        stack = jnp.concatenate([high, value - high], axis=0).astype(BF16)
        acc = acc + mxu(jnp.concatenate([stack, stack], axis=1), b2[j])
    forcing[...] = (acc[0:40] + acc[40:80])[0:34]

    for cp in (*early_x, *early_y, *chunk.values(), *lists.values(), *returns.values(), *sums_out, *fields.values()):
        cp.wait_send()


def per_device(spectra, surface_wind, water_mask, send_rows, send_count, pick_slot, pick_weight, ocean_current):
    strips, owners = lax.axis_size("wave"), lax.axis_size("ocean")
    opts = pick_slot.shape[1]
    coef, wide, wown, wxy = (jnp.asarray(x) for x in constants())
    anywhere = pl.BlockSpec(memory_space=pl.ANY)
    copies = 12 + 3 * (owners - 1)

    def f32(*shape):
        return pltpu.VMEM(shape, F32)

    def i32(*shape):
        return pltpu.VMEM(shape, jnp.int32)

    return pl.pallas_call(
        functools.partial(interval, strips, owners, opts),
        name="interval",
        out_shape=(
            jax.ShapeDtypeStruct((34, opts), F32),
            jax.ShapeDtypeStruct((2, 1, 128), F32),
        ),
        in_specs=[pl.BlockSpec(memory_space=pltpu.SMEM)] + [anywhere] * 12,
        out_specs=(pl.BlockSpec(memory_space=pltpu.VMEM),) * 2,
        scratch_shapes=[
            f32(ND, NF, 128),
            f32(ND, NF, 128),
            f32(ND, NF, 128),
            f32(ND * NF, 128),
            f32(2, EDGE, 128),
            f32(2, 1, 128),
            i32(1, 128),
            i32(owners, CAP),
            i32(1, owners),
            i32(4, opts),
            f32(4, opts),
            f32(2, opts),
            f32(4, FP, 128),
            f32(160, 256),
            f32(160, 256),
            f32(3, NF, 128),
            f32(2, NF, 128),
            f32(256, 256),
            f32(256, 256),
            f32(256, 128),
            f32(4, FP, 128),
            f32(2, 8, 128),
            f32(2, 8, 128),
            f32(2, 8, 896),
            f32(2, 8, 896),
            f32(4, 80, 128),
            f32(4, 80, 128),
            i32(owners, 8, 128),
            i32(owners, 8, 128),
            f32(40, 128),
            f32(owners, 40, 128),
            f32(owners, 8, 128),
            f32(owners, 8, 128),
            pltpu.VMEM((owners, 128, opts), BF16),
            pltpu.VMEM((owners, 256, opts), BF16),
            pltpu.VMEM((16, opts), BF16),
            pltpu.SemaphoreType.DMA((12,)),
            pltpu.SemaphoreType.DMA((copies,)),
            pltpu.SemaphoreType.DMA((copies,)),
        ],
        compiler_params=pltpu.CompilerParams(collective_id=0, has_side_effects=True, vmem_limit_bytes=60 << 20),
    )(
        coef,
        spectra.reshape(ND, NF, 1, 128),
        spectra.reshape(ND * NF, 128),
        surface_wind,
        water_mask,
        send_rows,
        send_count.reshape(1, owners),
        pick_slot,
        pick_weight,
        ocean_current,
        wide,
        wown,
        wxy,
    )


def solution(mesh):
    in_specs = (
        P("wave", None, None, "ocean"),
        P(None, "wave", "ocean"),
        P("wave", "ocean"),
        P(None, ("wave", "ocean")),
        P(None, ("wave", "ocean")),
        P(None, ("wave", "ocean")),
        P(None, ("wave", "ocean")),
        P(None, ("wave", "ocean")),
    )
    out_specs = (P(None, ("wave", "ocean")), P(None, "wave", "ocean"))
    return jax.shard_map(per_device, mesh=mesh, in_specs=in_specs, out_specs=out_specs, check_vma=False)
```

```python
import functools

import jax
import jax.numpy as jnp
import ml_dtypes
import numpy as np
from jax import lax
from jax.experimental import pallas as pl
from jax.experimental.pallas import tpu as pltpu
from jax.sharding import PartitionSpec as P

ND = 36
NF = 36
FP = 40
DEPTHS = 16
CAP = 64
QUAD = 9
MESH = pl.DeviceIdType.MESH
F32 = jnp.float32
BF16 = jnp.bfloat16
HALVES = ((0, 16), (16, 20))
STEP = 3
ROWS = 74
CH = 34
EDGE = QUAD * 2 * NF


def host_tables():
    angles = (np.arange(ND) + 0.5) * (2.0 * np.pi / ND)
    cosine, sines = np.cos(angles), np.sin(angles)
    frequency = np.arange(NF)
    speeds = 0.7 * 1.1 ** (-frequency)
    ratios = 1.1 ** (frequency - (NF - 1.0))
    kappas = 0.02 * 1.1 ** (2.0 * frequency)
    depths = 0.25 * np.arange(DEPTHS)
    kernel = np.sqrt(kappas)[:, None] * np.exp(-2.0 * kappas[:, None] * depths[None, :])
    return cosine, sines, speeds, ratios, kernel


def split_rows(values):
    high = values.astype(ml_dtypes.bfloat16)
    low = (values - high.astype(np.float64)).astype(ml_dtypes.bfloat16)
    return np.concatenate([high, low], 0).astype(np.float32)


def projection(scale):
    _, _, _, ratios, kernel = host_tables()
    table = np.zeros((80, 256))

    def put(row, group, values):
        table[row, group * FP : group * FP + NF] = values * scale / ND

    for depth in range(DEPTHS):
        k = kernel[:, depth]
        for side in (0, 1):
            put(16 * side + depth, side, k)
            put(16 * side + depth, 2 + side, k * ratios)
            put(40 + 16 * side + depth, side, 0.3 * k * ratios)
    for side in (0, 1):
        put(32 + side, 4 + side, ratios)
        put(72 + side, 2 + side, 0.3 * ratios * ratios)
    return split_rows(table)


def constants():
    cosine, sines, speeds, ratios, _ = host_tables()
    ac, an = np.abs(cosine), np.abs(sines)
    coef = np.zeros((ND, 16))
    for i, column in enumerate((ac, an, cosine * ac, sines * ac, cosine * an, sines * an, cosine, sines, ac + an)):
        coef[:, i] = column
    wide = np.zeros((4, FP, 128))
    for i, column in enumerate((speeds, ratios, cosine, sines)):
        wide[i, :36] = column[:, None]
    return (
        coef.astype(np.float32),
        wide.astype(np.float32),
        projection(np.ones(NF)),
        projection(speeds),
    )


def mxu(a, b, dims=(((1,), (0,)), ((), ()))):
    return lax.dot_general(a, b, dims, preferred_element_type=F32)


def split(x):
    high = x.astype(BF16)
    return high, (x - high.astype(F32)).astype(BF16)


def interval(
    strips,
    owners,
    opts,
    coef_hbm,
    spectra,
    flat,
    wind_hbm,
    mask_hbm,
    rows_hbm,
    count_hbm,
    pick_hbm,
    weight_hbm,
    current_hbm,
    wide_hbm,
    wown_hbm,
    wxy_hbm,
    forcing,
    back,
    coef,
    e_v,
    ex_v,
    m_v,
    flat_v,
    edge_v,
    wind,
    mask,
    rows,
    count,
    pick,
    weight,
    current,
    wide,
    wown,
    wxy,
    drive,
    ax_v,
    ay_v,
    xq,
    yq,
    oq,
    xs,
    xr,
    ys,
    yr,
    ps,
    pr,
    rs,
    rr,
    fs,
    fr,
    ts,
    tr,
    m2,
    b2,
    car,
    local_sem,
    send_sem,
    recv_sem,
):
    w, o = lax.axis_index("wave"), lax.axis_index("ocean")
    xp, xm = (lax.rem(w + 1, strips), o), (lax.rem(w + strips - 1, strips), o)
    yp, ym = (w, lax.rem(o + 1, owners)), (w, lax.rem(o + owners - 1, owners))

    def peer(j):
        return (w, lax.rem(o + j, owners))

    far_first = sorted(range(1, owners), key=lambda j: -min(j, owners - j))

    has_left, has_right = w > 0, w < strips - 1

    barrier = pltpu.get_barrier_semaphore()

    def greet(device):
        pl.semaphore_signal(barrier, inc=1, device_id=device, device_id_type=MESH)

    pl.when(has_right)(lambda: greet(xp))
    pl.when(has_left)(lambda: greet(xm))
    for j in far_first:
        greet(peer(j))

    loads = []
    for src, dst in (
        (spectra.at[:, :, 0, :], e_v),
        (coef_hbm, coef),
        (wind_hbm, wind),
        (wide_hbm, wide),
        (flat, flat_v),
        (rows_hbm, rows),
        (count_hbm, count),
        (mask_hbm, mask),
        (pick_hbm, pick),
        (weight_hbm, weight),
        (current_hbm, current),
        (wxy_hbm, wxy),
        (wown_hbm, wown),
    ):
        cp = pltpu.make_async_copy(src, dst, local_sem.at[len(loads)])
        cp.start()
        loads.append(cp)

    used = [0]

    def send(src, dst, device, there=None, back=None):
        i = used[0]
        used[0] += 1
        cp = pltpu.make_async_remote_copy(
            src_ref=src, dst_ref=dst, send_sem=send_sem.at[i], recv_sem=recv_sem.at[i], device_id=device, device_id_type=MESH
        )

        def under(condition, action):
            if condition is None:
                action()
            else:
                pl.when(condition)(action)

        under(there, cp.start)
        return lambda: under(back, cp.wait_recv), lambda: under(there, cp.wait_send)

    def to_right(src, dst):
        return send(src, dst, xp, has_right, has_left)

    def to_left(src, dst):
        return send(src, dst, xm, has_left, has_right)

    down_in = jnp.where(o > 0, 1.0, 0.0).astype(F32)
    up_in = jnp.where(o < owners - 1, 1.0, 0.0).astype(F32)
    lane = lax.broadcasted_iota(jnp.int32, (1, 128), 1)

    for ref in (xq, yq, oq):
        ref[...] = jnp.zeros(ref.shape, F32)
    ax_v[...] = jnp.zeros(ax_v.shape, F32)
    ay_v[...] = jnp.zeros(ay_v.shape, F32)

    @pl.when(jnp.logical_not(has_left))
    def _():
        ex_v[0:QUAD] = jnp.zeros((QUAD, NF, 128), F32)
        ex_v[3 * QUAD : ND] = jnp.zeros((QUAD, NF, 128), F32)
        xr[0] = jnp.zeros((8, 128), F32)
        pr[0] = jnp.zeros((ROWS, 128), F32)

    @pl.when(jnp.logical_not(has_right))
    def _():
        ex_v[QUAD : 3 * QUAD] = jnp.zeros((2 * QUAD, NF, 128), F32)
        xr[1] = jnp.zeros((8, 128), F32)
        pr[1] = jnp.zeros((ROWS, 128), F32)

    pl.semaphore_wait(barrier, owners - 1 + has_left.astype(jnp.int32) + has_right.astype(jnp.int32))
    order = []
    for i in range(0, QUAD, STEP):
        order += [(0, i), (2, i)]
    for i in range(0, QUAD, STEP):
        order += [(3, i), (1, i)]
    chunk = {}

    def send_chunks(which):
        for q, i in which:
            part = pl.ds(q * QUAD + i, STEP)
            chunk[q, i] = (to_right if q in (0, 3) else to_left)(spectra.at[part, :, 0, :], ex_v.at[part])

    send_chunks(order[:4])

    for cp in loads[:4]:
        cp.wait()
    s_all, r_all = wide[0, 0:NF, :], wide[1, 0:NF, :]
    sums = []
    for q in range(4):

        def gather_energy(i, acc, q=q):
            d = q * QUAD + i
            e = e_v[d]
            return acc[0] + e, acc[1] + coef[d, 0] * e, acc[2] + coef[d, 1] * e

        zero = jnp.zeros((NF, 128), F32)
        sums.append(lax.fori_loop(0, QUAD, gather_energy, (zero, zero, zero), unroll=3))

    def over_f(x):
        return jnp.sum(x, axis=0, keepdims=True)

    gc = [x[1] for x in sums]
    gn = [x[2] for x in sums]
    en_xp, en_xm = over_f(s_all * (gc[0] + gc[3])), over_f(s_all * (gc[1] + gc[2]))
    en_yp, en_ym = over_f(s_all * (gn[0] + gn[1])), over_f(s_all * (gn[2] + gn[3]))
    en_own = over_f(sums[0][0] + sums[1][0] + sums[2][0] + sums[3][0]) - (en_xp + en_xm + en_yp + en_ym)
    en_yp, en_ym = pltpu.roll(en_yp, 1, 1), pltpu.roll(en_ym, 127, 1)

    w0, w1 = wind[0], wind[1]
    row8 = lax.broadcasted_iota(jnp.int32, (8, 128), 0)

    def tile(energy):
        return jnp.where(row8 == 0, energy, jnp.where(row8 == 1, w0, w1))

    xs[0], xs[1] = tile(en_xp), tile(en_xm)

    early = [to_right(xs.at[0], xr.at[0]), to_left(xs.at[1], xr.at[1])]
    send_chunks(order[4:])

    for cp in loads[4:]:
        cp.wait()
    for side, last in ((0, 127), (1, 0)):
        pickup = jnp.where(lax.broadcasted_iota(jnp.int32, (16, 128), 1) == last, 1.0, 0.0).astype(BF16)
        high, low = split(flat_v[pl.ds(side * EDGE, EDGE), :])
        turned = (((1,), (1,)), ((), ()))
        ys[side, :, 0:128] = tile(en_yp if side == 0 else en_ym)
        ys[side, :, 128 : 128 + EDGE] = (mxu(pickup, high, turned) + mxu(pickup, low, turned))[0:8]
        ys[side, :, 128 + EDGE : 896] = jnp.zeros((8, 768 - EDGE), F32)
    early += [send(ys.at[0], yr.at[0], yp), send(ys.at[1], yr.at[1], ym)]

    lane8 = lax.broadcasted_iota(jnp.int32, (1, owners), 1)
    for j in range(owners):
        to = lax.rem(o + j, owners)
        picked = rows[pl.ds(to, 1), :]
        live = jnp.sum(jnp.where(lane8 == to, count[...], 0).astype(F32), axis=1, keepdims=True).astype(jnp.int32)
        both = jnp.concatenate([picked, picked], axis=1)
        rs[j] = jnp.where(row8 == 0, both, jnp.broadcast_to(live, (8, 128)))
    lists = {j: send(rs.at[j], rr.at[j], peer(j)) for j in far_first}
    rr[0] = rs[0]

    for j in range(owners):
        source = lax.rem(o + owners - j, owners)
        slots = lax.broadcasted_iota(jnp.int32, (CAP, opts), 0) + source * CAP
        total = jnp.zeros((CAP, opts), F32)
        for k in range(4):
            total = total + jnp.where(pick[k : k + 1, :] == slots, weight[k : k + 1, :], 0.0)
        high, low = split(total)
        m2[j, 0:CAP, :] = high
        m2[j, CAP : 2 * CAP, :] = low

    for arrive, _ in early:
        arrive()
    ct, nt = wide[2, 0:NF, :], wide[3, 0:NF, :]

    def driving(a, b):
        return 0.1 * jnp.maximum(a * ct + b * nt, 0.0)

    drive[0] = driving(w0, w1)
    drive[1] = jnp.where(
        ct > 0, driving(xr[1, 1:2, :], xr[1, 2:3, :]), driving(xr[0, 1:2, :], xr[0, 2:3, :])
    )
    up0 = jnp.where(lane == 127, pltpu.roll(yr[1, 1:2, 0:128], 127, 1), pltpu.roll(w0, 127, 1))
    up1 = jnp.where(lane == 127, pltpu.roll(yr[1, 2:3, 0:128], 127, 1), pltpu.roll(w1, 127, 1))
    dn0 = jnp.where(lane == 0, pltpu.roll(yr[0, 1:2, 0:128], 1, 1), pltpu.roll(w0, 1, 1))
    dn1 = jnp.where(lane == 0, pltpu.roll(yr[0, 2:3, 0:128], 1, 1), pltpu.roll(w1, 1, 1))
    drive[2] = jnp.where(nt > 0, driving(up0, up1), driving(dn0, dn1))
    energy = (
        en_own
        + xr[0, 0:1, :]
        + xr[1, 0:1, :]
        + jnp.where(lane == 0, down_in * yr[0, 0:1, 0:128], en_yp)
        + jnp.where(lane == 127, up_in * yr[1, 0:1, 0:128], en_ym)
    ) * (1.0 / (ND * NF))
    damp = 0.3 * (energy / (energy + 1.0))

    for side, (last, inside, shift) in enumerate(((0, down_in, 1), (127, up_in, 127))):
        place = jnp.where(lax.broadcasted_iota(jnp.int32, (16, 128), 1) == last, 1.0, 0.0)
        place = jnp.where(lax.rem(lax.broadcasted_iota(jnp.int32, (16, 128), 0), 8) == 0, place, 0.0).astype(BF16)
        high, low = split(yr[side, :, 128 : 128 + EDGE] * inside)
        both = jnp.concatenate([high.astype(F32), low.astype(F32)], axis=0).astype(BF16)
        edge_v[side] = mxu(both, place, (((0,), (0,)), ((), ())))
        for half in (0, 1):
            for i in range(QUAD):
                d = side * 2 * QUAD + half * QUAD + i
                e = e_v[d]
                k = (half * QUAD + i) * NF
                behind = jnp.where(lane == last, edge_v[side, k : k + NF, :], pltpu.roll(e, shift, 1))
                m_v[d] = e + s_all * (coef[d, 1] * behind - coef[d, 8] * e)

    carried = current[...]
    ones = jnp.ones((1, opts), F32)
    c_high = carried.astype(BF16).astype(F32)
    none = jnp.zeros((5, opts), F32)
    car[...] = jnp.concatenate([c_high, ones, none, carried - c_high, jnp.zeros((6, opts), F32)], axis=0).astype(BF16)
    point = lax.broadcasted_iota(jnp.int32, (128, 128), 0)
    slot = lax.rem(lax.broadcasted_iota(jnp.int32, (1, 128), 1), CAP)
    for j in range(owners):
        if j:
            lists[j][0]()
        hit = jnp.logical_and(rr[j, 0:1, :] == point, slot < rr[j, 1:2, :])
        matrix = mxu(jnp.where(hit, 1.0, 0.0).astype(BF16), m2[j])
        high, low = split(matrix)
        b2[j, 0:128, :] = high
        b2[j, 128:256, :] = low
        t = mxu(car[...], b2[j], (((1,), (1,)), ((), ())))
        ts[j] = t[0:8, 0:128] + t[8:16, 0:128] + t[0:8, 128:256] + t[8:16, 128:256]
    returns = {j: send(ts.at[j], tr.at[j], peer(owners - j)) for j in far_first}

    for q, first in order:
        chunk[q, first][0]()
        x_side, y_side = (0 if q in (0, 3) else 1), (0 if q in (0, 1) else 1)
        for low, n in HALVES:
            part = pl.ds(low, n)
            r, s = wide[1, part, :], wide[0, part, :]
            acc = [ref[side, g, part, :] for ref, side in ((ax_v, x_side), (ay_v, y_side)) for g in range(7)]
            for i in range(STEP):
                d = q * QUAD + first + i
                moved = m_v[d, part, :] + s * (coef[d, 0] * ex_v[d, part, :])
                e = moved + moved * (r * (drive[0, d : d + 1, :] - damp))
                m_v[d, part, :] = e
                out = []
                for at, (a, kc, kn) in ((1, (0, 2, 3)), (2, (1, 4, 5))):
                    here = drive[at, d : d + 1, :]
                    e1 = e * here
                    e2 = e1 * here
                    a, kc, kn = coef[d, a], coef[d, kc], coef[d, kn]
                    out += [a * e, kc * e, kn * e, kc * e1, kn * e1, kc * e2, kn * e2]
                acc = [x + y for x, y in zip(acc, out)]
            for ref, side, values in ((ax_v, x_side, acc[:7]), (ay_v, y_side, acc[7:])):
                for g, value in enumerate(values):
                    ref[side, g, part, :] = value

    sea = mask[...].astype(F32)

    def contract(table, x):
        high, low = split(x)
        both = table[...].astype(BF16)
        out = mxu(both, high)
        return out[0:80] + out[80:160] + mxu(both[0:80], low)

    def finish(value, energy_row):
        tail = value[32:40] + jnp.where(row8 == 2, energy_row, 0.0)
        return (sea * jnp.concatenate([value[0:32], tail, value[40:80]], axis=0))[0:ROWS]

    s_pad, r_pad = wide[0], wide[1]
    sums_out = []
    for acc_v, q_v, at in ((ax_v, xq, 0), (ay_v, yq, 2)):
        for side in (0, 1):
            col = pl.ds(side * 128, 128)
            for g in range(4):
                q_v[g * FP : (g + 1) * FP, col] = acc_v[side, g + 1]
            for g in (4, 5):
                q_v[g * FP : (g + 1) * FP, col] = acc_v[side, g - 1] + r_pad * acc_v[side, g + 1]
        out = contract(wxy, q_v[...])
        for side in (0, 1):
            value = finish(out[:, side * 128 : side * 128 + 128], over_f(s_pad * acc_v[side, 0]))
            ps[at + side] = value if at == 0 else pltpu.roll(value, (1, 127)[side], 1)
        if at == 0:
            sums_out += [to_right(ps.at[0], pr.at[0]), to_left(ps.at[1], pr.at[1])]
        else:
            sums_out += [send(ps.at[2], pr.at[2], yp), send(ps.at[3], pr.at[3], ym)]

    e_own = []
    for low, n in HALVES:
        part = pl.ds(low, n)
        r, s = wide[1, part, :], wide[0, part, :]

        def own_bins(d, acc, part=part, s=s):
            e = m_v[d, part, :]
            e = e - s * (coef[d, 8] * e)
            here = drive[0, pl.ds(d, 1), :]
            e1 = e * here
            e2 = e1 * here
            kc, kn = coef[d, 6], coef[d, 7]
            out = (e, kc * e, kn * e, kc * e1, kn * e1, kc * e2, kn * e2)
            return tuple(x + y for x, y in zip(acc, out))

        a = lax.fori_loop(0, ND, own_bins, (jnp.zeros((n, 128), F32),) * 7, unroll=4)
        for g, value in enumerate([a[1], a[2], a[3], a[4], a[3] + r * a[5], a[4] + r * a[6]]):
            oq[pl.ds(g * FP + low, n), :] = value
        e_own.append(over_f(a[0]))
    total = finish(contract(wown, oq[...]), e_own[0] + e_own[1])

    for j in range(1, owners):
        returns[j][0]()
    got = ts[0]
    for j in range(1, owners):
        got = got + tr[j]
    back[:, 0, :] = got[0:2] / jnp.maximum(got[2:3], 1.0)

    for arrive, _ in sums_out:
        arrive()
    total = (
        total
        + pr[0]
        + pr[1]
        + jnp.where(lane == 0, down_in * pr[2], ps[2])
        + jnp.where(lane == 127, up_in * pr[3], ps[3])
    )
    energy = total[34:35] * (1.0 / (ND * NF))
    fs[...] = sea * (total[0:CH] - (energy / (energy + 1.0)) * total[40:ROWS])
    fields = {j: send(fs, fr.at[j], peer(j)) for j in far_first}

    acc = jnp.zeros((80, opts), F32)
    for j in range(owners):
        if j:
            fields[j][0]()
        value = jnp.concatenate([fr[j] if j else fs[...], jnp.zeros((40 - CH, 128), F32)], axis=0)
        high = value.astype(BF16).astype(F32)
        stack = jnp.concatenate([high, value - high], axis=0).astype(BF16)
        acc = acc + mxu(jnp.concatenate([stack, stack], axis=1), b2[j])
    forcing[...] = (acc[0:40] + acc[40:80])[0:34]

    for _, leave in (*early, *chunk.values(), *lists.values(), *returns.values(), *sums_out, *fields.values()):
        leave()


def per_device(spectra, surface_wind, water_mask, send_rows, send_count, pick_slot, pick_weight, ocean_current):
    strips, owners = lax.axis_size("wave"), lax.axis_size("ocean")
    opts = pick_slot.shape[1]
    coef, wide, wown, wxy = (jnp.asarray(x) for x in constants())
    anywhere = pl.BlockSpec(memory_space=pltpu.HBM)
    copies = 8 + ND // STEP + 3 * (owners - 1)

    def f32(*shape):
        return pltpu.VMEM(shape, F32)

    def i32(*shape):
        return pltpu.VMEM(shape, jnp.int32)

    return pl.pallas_call(
        functools.partial(interval, strips, owners, opts),
        name="interval",
        out_shape=(
            jax.ShapeDtypeStruct((34, opts), F32),
            jax.ShapeDtypeStruct((2, 1, 128), F32),
        ),
        in_specs=[anywhere] * 13,
        out_specs=(pl.BlockSpec(memory_space=pltpu.VMEM),) * 2,
        scratch_shapes=[
            pltpu.SMEM((ND, 16), F32),
            f32(ND, NF, 128),
            f32(ND, NF, 128),
            f32(ND, NF, 128),
            f32(ND * NF, 128),
            f32(2, EDGE, 128),
            f32(2, 1, 128),
            i32(1, 128),
            i32(owners, CAP),
            i32(1, owners),
            i32(4, opts),
            f32(4, opts),
            f32(2, opts),
            f32(4, FP, 128),
            f32(160, 256),
            f32(160, 256),
            f32(3, NF, 128),
            f32(2, 7, FP, 128),
            f32(2, 7, FP, 128),
            f32(256, 256),
            f32(256, 256),
            f32(256, 128),
            f32(2, 8, 128),
            f32(2, 8, 128),
            f32(2, 8, 896),
            f32(2, 8, 896),
            f32(4, ROWS, 128),
            f32(4, ROWS, 128),
            i32(owners, 8, 128),
            i32(owners, 8, 128),
            f32(CH, 128),
            f32(owners, CH, 128),
            f32(owners, 8, 128),
            f32(owners, 8, 128),
            pltpu.VMEM((owners, 128, opts), BF16),
            pltpu.VMEM((owners, 256, opts), BF16),
            pltpu.VMEM((16, opts), BF16),
            pltpu.SemaphoreType.DMA((13,)),
            pltpu.SemaphoreType.DMA((copies,)),
            pltpu.SemaphoreType.DMA((copies,)),
        ],
        compiler_params=pltpu.CompilerParams(collective_id=0, has_side_effects=True, vmem_limit_bytes=32 << 20),
    )(
        *(
            pltpu.with_memory_space_constraint(x, pltpu.HBM)
            for x in (
                coef,
                spectra.reshape(ND, NF, 1, 128),
                spectra.reshape(ND * NF, 128),
                surface_wind,
                water_mask,
                send_rows,
                send_count.reshape(1, owners),
                pick_slot,
                pick_weight,
                ocean_current,
                wide,
                wown,
                wxy,
            )
        )
    )


def solution(mesh):
    in_specs = (
        P("wave", None, None, "ocean"),
        P(None, "wave", "ocean"),
        P("wave", "ocean"),
        P(None, ("wave", "ocean")),
        P(None, ("wave", "ocean")),
        P(None, ("wave", "ocean")),
        P(None, ("wave", "ocean")),
        P(None, ("wave", "ocean")),
    )
    out_specs = (P(None, ("wave", "ocean")), P(None, "wave", "ocean"))
    return jax.shard_map(per_device, mesh=mesh, in_specs=in_specs, out_specs=out_specs, check_vma=False)
```

```python
import functools

import jax
import jax.numpy as jnp
import ml_dtypes
import numpy as np
from jax import lax
from jax.experimental import pallas as pl
from jax.experimental.pallas import tpu as pltpu
from jax.sharding import PartitionSpec as P

ND = 36
NF = 36
FP = 40
DEPTHS = 16
CAP = 64
QUAD = 9
MESH = pl.DeviceIdType.MESH
F32 = jnp.float32
BF16 = jnp.bfloat16
HALVES = ((0, 16), (16, 20))
STEP = 3
ROWS = 74
CH = 34
EDGE = QUAD * 2 * NF


def host_tables():
    angles = (np.arange(ND) + 0.5) * (2.0 * np.pi / ND)
    cosine, sines = np.cos(angles), np.sin(angles)
    frequency = np.arange(NF)
    speeds = 0.7 * 1.1 ** (-frequency)
    ratios = 1.1 ** (frequency - (NF - 1.0))
    kappas = 0.02 * 1.1 ** (2.0 * frequency)
    depths = 0.25 * np.arange(DEPTHS)
    kernel = np.sqrt(kappas)[:, None] * np.exp(-2.0 * kappas[:, None] * depths[None, :])
    return cosine, sines, speeds, ratios, kernel


def split_rows(values):
    high = values.astype(ml_dtypes.bfloat16)
    low = (values - high.astype(np.float64)).astype(ml_dtypes.bfloat16)
    return np.concatenate([high, low], 0).astype(np.float32)


def projection(scale):
    _, _, _, ratios, kernel = host_tables()
    table = np.zeros((80, 256))

    def put(row, group, values):
        table[row, group * FP : group * FP + NF] = values * scale / ND

    for depth in range(DEPTHS):
        k = kernel[:, depth]
        for side in (0, 1):
            put(16 * side + depth, side, k)
            put(16 * side + depth, 2 + side, k * ratios)
            put(40 + 16 * side + depth, side, 0.3 * k * ratios)
    for side in (0, 1):
        put(32 + side, 4 + side, ratios)
        put(72 + side, 2 + side, 0.3 * ratios * ratios)
    return split_rows(table)


def constants():
    cosine, sines, speeds, ratios, _ = host_tables()
    ac, an = np.abs(cosine), np.abs(sines)
    coef = np.zeros((ND, 16))
    for i, column in enumerate((ac, an, cosine * ac, sines * ac, cosine * an, sines * an, cosine, sines, ac + an)):
        coef[:, i] = column
    wide = np.zeros((4, FP, 128))
    for i, column in enumerate((speeds, ratios, cosine, sines)):
        wide[i, :36] = column[:, None]
    return (
        coef.astype(np.float32),
        wide.astype(np.float32),
        projection(np.ones(NF)),
        projection(speeds),
    )


def mxu(a, b, dims=(((1,), (0,)), ((), ()))):
    return lax.dot_general(a, b, dims, preferred_element_type=F32)


def split(x):
    high = x.astype(BF16)
    return high, (x - high.astype(F32)).astype(BF16)


def interval(
    strips,
    owners,
    opts,
    coef_hbm,
    spectra,
    flat,
    wind_hbm,
    mask_hbm,
    rows_hbm,
    count_hbm,
    pick_hbm,
    weight_hbm,
    current_hbm,
    wide_hbm,
    wown_hbm,
    wxy_hbm,
    forcing,
    back,
    coef,
    e_v,
    ex_v,
    m_v,
    flat_v,
    edge_v,
    wind,
    mask,
    rows,
    count,
    pick,
    weight,
    current,
    wide,
    wown,
    wxy,
    drive,
    ax_v,
    ay_v,
    oq,
    xs,
    xr,
    ys,
    yr,
    ps,
    pr,
    fs,
    fr,
    ts,
    tr,
    m2,
    all_slots,
    live_slots,
    local_sem,
    send_sem,
    recv_sem,
):
    w, o = lax.axis_index("wave"), lax.axis_index("ocean")
    xp, xm = (lax.rem(w + 1, strips), o), (lax.rem(w + strips - 1, strips), o)
    yp, ym = (w, lax.rem(o + 1, owners)), (w, lax.rem(o + owners - 1, owners))

    def peer(j):
        return (w, lax.rem(o + j, owners))

    far_first = sorted(range(1, owners), key=lambda j: -min(j, owners - j))

    has_left, has_right = w > 0, w < strips - 1

    barrier = pltpu.get_barrier_semaphore()

    def greet(device):
        pl.semaphore_signal(barrier, inc=1, device_id=device, device_id_type=MESH)

    pl.when(has_right)(lambda: greet(xp))
    pl.when(has_left)(lambda: greet(xm))
    for j in far_first:
        greet(peer(j))

    loads = []
    for src, dst in (
        (spectra.at[:, :, 0, :], e_v),
        (coef_hbm, coef),
        (wind_hbm, wind),
        (wide_hbm, wide),
        (flat, flat_v),
        (rows_hbm, rows),
        (count_hbm, count),
        (mask_hbm, mask),
        (pick_hbm, pick),
        (weight_hbm, weight),
        (current_hbm, current),
        (wxy_hbm, wxy),
        (wown_hbm, wown),
    ):
        cp = pltpu.make_async_copy(src, dst, local_sem.at[len(loads)])
        cp.start()
        loads.append(cp)

    used = [0]

    def send(src, dst, device, there=None, back=None):
        i = used[0]
        used[0] += 1
        cp = pltpu.make_async_remote_copy(
            src_ref=src, dst_ref=dst, send_sem=send_sem.at[i], recv_sem=recv_sem.at[i], device_id=device, device_id_type=MESH
        )

        def under(condition, action):
            if condition is None:
                action()
            else:
                pl.when(condition)(action)

        under(there, cp.start)
        return lambda: under(back, cp.wait_recv), lambda: under(there, cp.wait_send)

    def to_right(src, dst):
        return send(src, dst, xp, has_right, has_left)

    def to_left(src, dst):
        return send(src, dst, xm, has_left, has_right)

    down_in = jnp.where(o > 0, 1.0, 0.0).astype(F32)
    up_in = jnp.where(o < owners - 1, 1.0, 0.0).astype(F32)
    lane = lax.broadcasted_iota(jnp.int32, (1, 128), 1)

    oq[...] = jnp.zeros(oq.shape, F32)
    ax_v[...] = jnp.zeros(ax_v.shape, F32)
    ay_v[...] = jnp.zeros(ay_v.shape, F32)

    @pl.when(jnp.logical_not(has_left))
    def _():
        ex_v[0:QUAD] = jnp.zeros((QUAD, NF, 128), F32)
        ex_v[3 * QUAD : ND] = jnp.zeros((QUAD, NF, 128), F32)
        xr[0] = jnp.zeros((8, 128), F32)
        pr[0] = jnp.zeros((ROWS, 128), F32)

    @pl.when(jnp.logical_not(has_right))
    def _():
        ex_v[QUAD : 3 * QUAD] = jnp.zeros((2 * QUAD, NF, 128), F32)
        xr[1] = jnp.zeros((8, 128), F32)
        pr[1] = jnp.zeros((ROWS, 128), F32)

    for cp in loads[:5]:
        cp.wait()
    s_all, r_all = wide[0, 0:NF, :], wide[1, 0:NF, :]
    sums = []
    for q in range(4):

        def gather_energy(i, acc, q=q):
            d = q * QUAD + i
            e = e_v[d]
            return acc[0] + e, acc[1] + coef[d, 0] * e, acc[2] + coef[d, 1] * e

        zero = jnp.zeros((NF, 128), F32)
        sums.append(lax.fori_loop(0, QUAD, gather_energy, (zero, zero, zero), unroll=3))

    def over_f(x):
        return jnp.sum(x, axis=0, keepdims=True)

    gc = [x[1] for x in sums]
    gn = [x[2] for x in sums]
    en_xp, en_xm = over_f(s_all * (gc[0] + gc[3])), over_f(s_all * (gc[1] + gc[2]))
    en_yp, en_ym = over_f(s_all * (gn[0] + gn[1])), over_f(s_all * (gn[2] + gn[3]))
    en_own = over_f(sums[0][0] + sums[1][0] + sums[2][0] + sums[3][0]) - (en_xp + en_xm + en_yp + en_ym)
    en_yp, en_ym = pltpu.roll(en_yp, 1, 1), pltpu.roll(en_ym, 127, 1)

    w0, w1 = wind[0], wind[1]
    row8 = lax.broadcasted_iota(jnp.int32, (8, 128), 0)

    def tile(energy):
        return jnp.where(row8 == 0, energy, jnp.where(row8 == 1, w0, w1))

    xs[0], xs[1] = tile(en_xp), tile(en_xm)

    for side, last in ((0, 127), (1, 0)):
        pickup = jnp.where(lax.broadcasted_iota(jnp.int32, (16, 128), 1) == last, 1.0, 0.0).astype(BF16)
        high, low = split(flat_v[pl.ds(side * EDGE, EDGE), :])
        turned = (((1,), (1,)), ((), ()))
        ys[side, :, 0:128] = tile(en_yp if side == 0 else en_ym)
        ys[side, :, 128 : 128 + EDGE] = (mxu(pickup, high, turned) + mxu(pickup, low, turned))[0:8]
        ys[side, :, 128 + EDGE : 896] = jnp.zeros((8, 768 - EDGE), F32)
    pl.semaphore_wait(barrier, owners - 1 + has_left.astype(jnp.int32) + has_right.astype(jnp.int32))
    early = [to_right(xs.at[0], xr.at[0]), to_left(xs.at[1], xr.at[1])]
    early += [send(ys.at[0], yr.at[0], yp), send(ys.at[1], yr.at[1], ym)]

    orders = [[(q, i) for q in side for i in range(0, QUAD, STEP)] for side in ((0, 3), (2, 1))]
    chunk = {}
    for pair in zip(*orders):
        for (q, i), towards in zip(pair, (to_right, to_left)):
            part = pl.ds(q * QUAD + i, STEP)
            chunk[q, i] = towards(e_v.at[part], ex_v.at[part])

    for cp in loads[5:]:
        cp.wait()

    lane8 = lax.broadcasted_iota(jnp.int32, (1, owners), 1)
    point = lax.broadcasted_iota(jnp.int32, (128, 128), 0)
    slot = lax.rem(lane, CAP)
    for j in range(owners):
        to = lax.rem(o + j, owners)
        picked = rows[pl.ds(to, 1), :]
        number = jnp.sum(jnp.where(lane8 == to, count[...], 0).astype(F32), axis=1, keepdims=True).astype(jnp.int32)
        hit = jnp.concatenate([picked, picked], axis=1) == point
        at = pl.ds(j * 128, 128)
        all_slots[:, at] = jnp.where(hit, 1.0, 0.0).astype(BF16)
        live_slots[:, at] = jnp.where(jnp.logical_and(hit, slot < number), 1.0, 0.0).astype(BF16)

    for j in range(owners):
        source = lax.rem(o + owners - j, owners)
        slots = lax.broadcasted_iota(jnp.int32, (CAP, opts), 0) + source * CAP
        total = jnp.zeros((CAP, opts), F32)
        for k in range(4):
            total = total + jnp.where(pick[k : k + 1, :] == slots, weight[k : k + 1, :], 0.0)
        high, low = split(total)
        m2[pl.ds(j * 128, CAP), :] = high
        m2[pl.ds(j * 128 + CAP, CAP), :] = low

    for arrive, _ in early:
        arrive()
    ct, nt = wide[2, 0:NF, :], wide[3, 0:NF, :]

    def driving(a, b):
        return 0.1 * jnp.maximum(a * ct + b * nt, 0.0)

    drive[0] = driving(w0, w1)
    drive[1] = jnp.where(
        ct > 0, driving(xr[1, 1:2, :], xr[1, 2:3, :]), driving(xr[0, 1:2, :], xr[0, 2:3, :])
    )
    up0 = jnp.where(lane == 127, pltpu.roll(yr[1, 1:2, 0:128], 127, 1), pltpu.roll(w0, 127, 1))
    up1 = jnp.where(lane == 127, pltpu.roll(yr[1, 2:3, 0:128], 127, 1), pltpu.roll(w1, 127, 1))
    dn0 = jnp.where(lane == 0, pltpu.roll(yr[0, 1:2, 0:128], 1, 1), pltpu.roll(w0, 1, 1))
    dn1 = jnp.where(lane == 0, pltpu.roll(yr[0, 2:3, 0:128], 1, 1), pltpu.roll(w1, 1, 1))
    drive[2] = jnp.where(nt > 0, driving(up0, up1), driving(dn0, dn1))
    energy = (
        en_own
        + xr[0, 0:1, :]
        + xr[1, 0:1, :]
        + jnp.where(lane == 0, down_in * yr[0, 0:1, 0:128], en_yp)
        + jnp.where(lane == 127, up_in * yr[1, 0:1, 0:128], en_ym)
    ) * (1.0 / (ND * NF))
    damp = 0.3 * (energy / (energy + 1.0))

    for side, (last, inside, shift) in enumerate(((0, down_in, 1), (127, up_in, 127))):
        place = jnp.where(lax.broadcasted_iota(jnp.int32, (16, 128), 1) == last, 1.0, 0.0)
        place = jnp.where(lax.rem(lax.broadcasted_iota(jnp.int32, (16, 128), 0), 8) == 0, place, 0.0).astype(BF16)
        high, low = split(yr[side, :, 128 : 128 + EDGE] * inside)
        both = jnp.concatenate([high.astype(F32), low.astype(F32)], axis=0).astype(BF16)
        edge_v[side] = mxu(both, place, (((0,), (0,)), ((), ())))
        for half in (0, 1):
            for i in range(QUAD):
                d = side * 2 * QUAD + half * QUAD + i
                e = e_v[d]
                k = (half * QUAD + i) * NF
                behind = jnp.where(lane == last, edge_v[side, k : k + NF, :], pltpu.roll(e, shift, 1))
                m_v[d] = e + s_all * (coef[d, 1] * behind - coef[d, 8] * e)

    carried = current[...]
    ones = jnp.ones((1, opts), F32)
    c_high = carried.astype(BF16).astype(F32)
    none = jnp.zeros((5, opts), F32)
    car = jnp.concatenate([c_high, ones, none, carried - c_high, jnp.zeros((6, opts), F32)], axis=0).astype(BF16)
    t = mxu(car, m2[...], (((1,), (1,)), ((), ())))
    t = t[0:8] + t[8:16]
    for j in range(owners):
        part = t[:, j * 128 : j * 128 + 128]
        ts[j] = part + pltpu.roll(part, CAP, 1)
    returns = {j: send(ts.at[j], tr.at[j], peer(owners - j)) for j in far_first}

    sea = mask[...].astype(F32)
    s_pad, r_pad = wide[0], wide[1]

    def contract(table, x):
        high, low = split(x)
        both = table[...].astype(BF16)
        out = mxu(both, high)
        return out[0:80] + out[80:160] + mxu(both[0:80], low)

    def finish(value, energy_row):
        tail = value[32:40] + jnp.where(row8 == 2, energy_row, 0.0)
        return (sea * jnp.concatenate([value[0:32], tail, value[40:80]], axis=0))[0:ROWS]

    def project(acc_v, side):
        sums = [acc_v[side, g] for g in range(7)]
        parts = sums[1:5] + [sums[3] + r_pad * sums[5], sums[4] + r_pad * sums[6], jnp.zeros((16, 128), F32)]
        return finish(contract(wxy, jnp.concatenate(parts, axis=0)), over_f(s_pad * sums[0]))

    def advance(q, first):
        chunk[q, first][0]()
        x_side, y_side = (0 if q in (0, 3) else 1), (0 if q in (0, 1) else 1)
        for low, n in HALVES:
            part = pl.ds(low, n)
            r, s = wide[1, part, :], wide[0, part, :]
            acc = [ref[side, g, part, :] for ref, side in ((ax_v, x_side), (ay_v, y_side)) for g in range(7)]
            for i in range(STEP):
                d = q * QUAD + first + i
                moved = m_v[d, part, :] + s * (coef[d, 0] * ex_v[d, part, :])
                e = moved + moved * (r * (drive[0, d : d + 1, :] - damp))
                m_v[d, part, :] = e
                out = []
                for at, (a, kc, kn) in ((1, (0, 2, 3)), (2, (1, 4, 5))):
                    here = drive[at, d : d + 1, :]
                    e1 = e * here
                    e2 = e1 * here
                    a, kc, kn = coef[d, a], coef[d, kc], coef[d, kn]
                    out += [a * e, kc * e, kn * e, kc * e1, kn * e1, kc * e2, kn * e2]
                acc = [x + y for x, y in zip(acc, out)]
            for ref, side, values in ((ax_v, x_side, acc[:7]), (ay_v, y_side, acc[7:])):
                for g, value in enumerate(values):
                    ref[side, g, part, :] = value

    sums_out = []
    for side, towards in ((0, to_right), (1, to_left)):
        for q, first in orders[side]:
            advance(q, first)
        ps[side] = project(ax_v, side)
        sums_out.append(towards(ps.at[side], pr.at[side]))
    for side, device in ((0, yp), (1, ym)):
        ps[2 + side] = pltpu.roll(project(ay_v, side), (1, 127)[side], 1)
        sums_out.append(send(ps.at[2 + side], pr.at[2 + side], device))

    e_own = []
    for low, n in HALVES:
        part = pl.ds(low, n)
        r, s = wide[1, part, :], wide[0, part, :]

        def own_bins(d, acc, part=part, s=s):
            e = m_v[d, part, :]
            e = e - s * (coef[d, 8] * e)
            here = drive[0, pl.ds(d, 1), :]
            e1 = e * here
            e2 = e1 * here
            kc, kn = coef[d, 6], coef[d, 7]
            out = (e, kc * e, kn * e, kc * e1, kn * e1, kc * e2, kn * e2)
            return tuple(x + y for x, y in zip(acc, out))

        a = lax.fori_loop(0, ND, own_bins, (jnp.zeros((n, 128), F32),) * 7, unroll=4)
        for g, value in enumerate([a[1], a[2], a[3], a[4], a[3] + r * a[5], a[4] + r * a[6]]):
            oq[pl.ds(g * FP + low, n), :] = value
        e_own.append(over_f(a[0]))
    total = finish(contract(wown, oq[...]), e_own[0] + e_own[1])

    for j in range(1, owners):
        returns[j][0]()
    sums = []
    for j in range(owners):
        value = tr[j] if j else ts[0]
        high = value.astype(BF16).astype(F32)
        sums.append(jnp.where(lane < CAP, high, value - high))
    sums = jnp.concatenate(sums, axis=1)
    sums = jnp.concatenate([sums, jnp.zeros(sums.shape, F32)], axis=0).astype(BF16)
    got = mxu(sums, all_slots[...], (((1,), (1,)), ((), ())))
    back[:, 0, :] = got[0:2] / jnp.maximum(got[2:3], 1.0)

    for arrive, _ in sums_out:
        arrive()
    total = (
        total
        + pr[0]
        + pr[1]
        + jnp.where(lane == 0, down_in * pr[2], ps[2])
        + jnp.where(lane == 127, up_in * pr[3], ps[3])
    )
    energy = total[34:35] * (1.0 / (ND * NF))
    value = sea * (total[0:CH] - (energy / (energy + 1.0)) * total[40:ROWS])

    half = CH // 2
    gap = jnp.zeros((24 - half, 128), F32)

    def two_parts(x):
        high = x.astype(BF16).astype(F32)
        return jnp.concatenate([high, x - high], axis=0).astype(BF16)

    out = mxu(two_parts(jnp.concatenate([value[0:half], gap, value[half:CH], gap], axis=0)), live_slots[...])
    out = out[0:48] + out[48:96]
    fields = {}
    for j in far_first + [0]:
        at = slice(j * 128, j * 128 + 128)
        fs[j] = jnp.where(lane < CAP, out[0:half, at], out[24 : 24 + half, at])
        if j:
            fields[j] = send(fs.at[j], fr.at[j], peer(j))

    acc = jnp.zeros((96, opts), F32)
    for j in range(0, owners, 2):
        sides = []
        for k in (j, j + 1):
            if k:
                fields[k][0]()
            value = jnp.concatenate([fr[k] if k else fs[0], gap], axis=0)
            other = pltpu.roll(value, CAP, 1)
            sides.append(two_parts(jnp.concatenate([jnp.where(lane < CAP, value, other), jnp.where(lane < CAP, other, value)], axis=0)))
        acc = acc + mxu(jnp.concatenate(sides, axis=1), m2[j * 128 : j * 128 + 256, :])
    acc = acc[0:48] + acc[48:96]
    forcing[0:half, :] = acc[0:half]
    forcing[half:CH, :] = acc[24 : 24 + half]

    for _, leave in (*early, *chunk.values(), *returns.values(), *sums_out, *fields.values()):
        leave()


def per_device(spectra, surface_wind, water_mask, send_rows, send_count, pick_slot, pick_weight, ocean_current):
    strips, owners = lax.axis_size("wave"), lax.axis_size("ocean")
    opts = pick_slot.shape[1]
    coef, wide, wown, wxy = (jnp.asarray(x) for x in constants())
    anywhere = pl.BlockSpec(memory_space=pltpu.HBM)
    copies = 8 + ND // STEP + 2 * (owners - 1)

    def f32(*shape):
        return pltpu.VMEM(shape, F32)

    def i32(*shape):
        return pltpu.VMEM(shape, jnp.int32)

    return pl.pallas_call(
        functools.partial(interval, strips, owners, opts),
        name="interval",
        out_shape=(
            jax.ShapeDtypeStruct((34, opts), F32),
            jax.ShapeDtypeStruct((2, 1, 128), F32),
        ),
        in_specs=[anywhere] * 13,
        out_specs=(pl.BlockSpec(memory_space=pltpu.VMEM),) * 2,
        scratch_shapes=[
            pltpu.SMEM((ND, 16), F32),
            f32(ND, NF, 128),
            f32(ND, NF, 128),
            f32(ND, NF, 128),
            f32(ND * NF, 128),
            f32(2, EDGE, 128),
            f32(2, 1, 128),
            i32(1, 128),
            i32(owners, CAP),
            i32(1, owners),
            i32(4, opts),
            f32(4, opts),
            f32(2, opts),
            f32(4, FP, 128),
            f32(160, 256),
            f32(160, 256),
            f32(3, NF, 128),
            f32(2, 7, FP, 128),
            f32(2, 7, FP, 128),
            f32(256, 128),
            f32(2, 8, 128),
            f32(2, 8, 128),
            f32(2, 8, 896),
            f32(2, 8, 896),
            f32(4, ROWS, 128),
            f32(4, ROWS, 128),
            f32(owners, CH // 2, 128),
            f32(owners, CH // 2, 128),
            f32(owners, 8, 128),
            f32(owners, 8, 128),
            pltpu.VMEM((owners * 128, opts), BF16),
            pltpu.VMEM((128, owners * 128), BF16),
            pltpu.VMEM((128, owners * 128), BF16),
            pltpu.SemaphoreType.DMA((13,)),
            pltpu.SemaphoreType.DMA((copies,)),
            pltpu.SemaphoreType.DMA((copies,)),
        ],
        compiler_params=pltpu.CompilerParams(collective_id=0, has_side_effects=True, vmem_limit_bytes=32 << 20),
    )(
        *(
            pltpu.with_memory_space_constraint(x, pltpu.HBM)
            for x in (
                coef,
                spectra.reshape(ND, NF, 1, 128),
                spectra.reshape(ND * NF, 128),
                surface_wind,
                water_mask,
                send_rows,
                send_count.reshape(1, owners),
                pick_slot,
                pick_weight,
                ocean_current,
                wide,
                wown,
                wxy,
            )
        )
    )


def solution(mesh):
    in_specs = (
        P("wave", None, None, "ocean"),
        P(None, "wave", "ocean"),
        P("wave", "ocean"),
        P(None, ("wave", "ocean")),
        P(None, ("wave", "ocean")),
        P(None, ("wave", "ocean")),
        P(None, ("wave", "ocean")),
        P(None, ("wave", "ocean")),
    )
    out_specs = (P(None, ("wave", "ocean")), P(None, "wave", "ocean"))
    return jax.shard_map(per_device, mesh=mesh, in_specs=in_specs, out_specs=out_specs, check_vma=False)
```

```python
import functools

import jax
import jax.numpy as jnp
import ml_dtypes
import numpy as np
from jax import lax
from jax.experimental import pallas as pl
from jax.experimental.pallas import tpu as pltpu
from jax.sharding import PartitionSpec as P

ND = 36
NF = 36
FP = 40
DEPTHS = 16
CAP = 64
QUAD = 9
MESH = pl.DeviceIdType.MESH
F32 = jnp.float32
BF16 = jnp.bfloat16
HALVES = ((0, 16), (16, 20))
STEP = 3
AHEAD = 4
ROWS = 74
CH = 34
EDGE = QUAD * 2 * NF


def host_tables():
    angles = (np.arange(ND) + 0.5) * (2.0 * np.pi / ND)
    cosine, sines = np.cos(angles), np.sin(angles)
    frequency = np.arange(NF)
    speeds = 0.7 * 1.1 ** (-frequency)
    ratios = 1.1 ** (frequency - (NF - 1.0))
    kappas = 0.02 * 1.1 ** (2.0 * frequency)
    depths = 0.25 * np.arange(DEPTHS)
    kernel = np.sqrt(kappas)[:, None] * np.exp(-2.0 * kappas[:, None] * depths[None, :])
    return cosine, sines, speeds, ratios, kernel


def split_rows(values):
    high = values.astype(ml_dtypes.bfloat16)
    low = (values - high.astype(np.float64)).astype(ml_dtypes.bfloat16)
    return np.concatenate([high, low], 0).astype(np.float32)


def projection(scale):
    _, _, _, ratios, kernel = host_tables()
    table = np.zeros((80, 256))

    def put(row, group, values):
        table[row, group * FP : group * FP + NF] = values * scale / ND

    for depth in range(DEPTHS):
        k = kernel[:, depth]
        for side in (0, 1):
            put(16 * side + depth, side, k)
            put(16 * side + depth, 2 + side, k * ratios)
            put(40 + 16 * side + depth, side, 0.3 * k * ratios)
    for side in (0, 1):
        put(32 + side, 4 + side, ratios)
        put(72 + side, 2 + side, 0.3 * ratios * ratios)
    return split_rows(table)


def constants():
    cosine, sines, speeds, ratios, _ = host_tables()
    ac, an = np.abs(cosine), np.abs(sines)
    coef = np.zeros((ND, 16))
    for i, column in enumerate((ac, an, cosine * ac, sines * ac, cosine * an, sines * an, cosine, sines, ac + an)):
        coef[:, i] = column
    wide = np.zeros((4, FP, 128))
    for i, column in enumerate((speeds, ratios, cosine, sines)):
        wide[i, :36] = column[:, None]
    return (
        coef.astype(np.float32),
        wide.astype(np.float32),
        projection(np.ones(NF)),
        projection(speeds),
    )


def mxu(a, b, dims=(((1,), (0,)), ((), ()))):
    return lax.dot_general(a, b, dims, preferred_element_type=F32)


def split(x):
    high = x.astype(BF16)
    return high, (x - high.astype(F32)).astype(BF16)


def interval(
    strips,
    owners,
    opts,
    coef_hbm,
    spectra,
    flat,
    wind_hbm,
    mask_hbm,
    rows_hbm,
    count_hbm,
    pick_hbm,
    weight_hbm,
    current_hbm,
    wide_hbm,
    wown_hbm,
    wxy_hbm,
    forcing,
    back,
    coef,
    e_v,
    ex_v,
    m_v,
    flat_v,
    edge_v,
    wind,
    mask,
    rows,
    count,
    pick,
    weight,
    current,
    wide,
    wown,
    wxy,
    drive,
    ax_v,
    ay_v,
    oq,
    xs,
    xr,
    ys,
    yr,
    ps,
    pr,
    fs,
    fr,
    ts,
    tr,
    m2,
    all_slots,
    live_slots,
    local_sem,
    send_sem,
    recv_sem,
):
    w, o = lax.axis_index("wave"), lax.axis_index("ocean")
    xp, xm = (lax.rem(w + 1, strips), o), (lax.rem(w + strips - 1, strips), o)
    yp, ym = (w, lax.rem(o + 1, owners)), (w, lax.rem(o + owners - 1, owners))

    def peer(j):
        return (w, lax.rem(o + j, owners))

    far_first = sorted(range(1, owners), key=lambda j: -min(j, owners - j))

    has_left, has_right = w > 0, w < strips - 1

    barrier = pltpu.get_barrier_semaphore()

    def greet(device):
        pl.semaphore_signal(barrier, inc=1, device_id=device, device_id_type=MESH)

    pl.when(has_right)(lambda: greet(xp))
    pl.when(has_left)(lambda: greet(xm))
    for j in far_first:
        greet(peer(j))

    loads = []
    for src, dst in (
        (spectra.at[:, :, 0, :], e_v),
        (coef_hbm, coef),
        (wind_hbm, wind),
        (wide_hbm, wide),
        (flat, flat_v),
        (rows_hbm, rows),
        (count_hbm, count),
        (mask_hbm, mask),
        (pick_hbm, pick),
        (weight_hbm, weight),
        (current_hbm, current),
        (wxy_hbm, wxy),
        (wown_hbm, wown),
    ):
        cp = pltpu.make_async_copy(src, dst, local_sem.at[len(loads)])
        cp.start()
        loads.append(cp)

    used = [0]

    def send(src, dst, device, there=None, back=None):
        i = used[0]
        used[0] += 1
        cp = pltpu.make_async_remote_copy(
            src_ref=src, dst_ref=dst, send_sem=send_sem.at[i], recv_sem=recv_sem.at[i], device_id=device, device_id_type=MESH
        )

        def under(condition, action):
            if condition is None:
                action()
            else:
                pl.when(condition)(action)

        under(there, cp.start)
        return lambda: under(back, cp.wait_recv), lambda: under(there, cp.wait_send)

    def to_right(src, dst):
        return send(src, dst, xp, has_right, has_left)

    def to_left(src, dst):
        return send(src, dst, xm, has_left, has_right)

    def to_up(src, dst):
        return send(src, dst, yp)

    def to_down(src, dst):
        return send(src, dst, ym)

    down_in = jnp.where(o > 0, 1.0, 0.0).astype(F32)
    up_in = jnp.where(o < owners - 1, 1.0, 0.0).astype(F32)
    lane = lax.broadcasted_iota(jnp.int32, (1, 128), 1)

    oq[...] = jnp.zeros(oq.shape, F32)
    ax_v[...] = jnp.zeros(ax_v.shape, F32)
    ay_v[...] = jnp.zeros(ay_v.shape, F32)

    @pl.when(jnp.logical_not(has_left))
    def _():
        ex_v[0:QUAD] = jnp.zeros((QUAD, NF, 128), F32)
        ex_v[3 * QUAD : ND] = jnp.zeros((QUAD, NF, 128), F32)
        xr[0] = jnp.zeros((8, 128), F32)
        pr[0] = jnp.zeros((ROWS, 128), F32)

    @pl.when(jnp.logical_not(has_right))
    def _():
        ex_v[QUAD : 3 * QUAD] = jnp.zeros((2 * QUAD, NF, 128), F32)
        xr[1] = jnp.zeros((8, 128), F32)
        pr[1] = jnp.zeros((ROWS, 128), F32)

    order = [(q, i) for pair in ((0, 2), (3, 1)) for i in range(0, QUAD, STEP) for q in pair]
    chunk = {}

    def send_chunks(which):
        for q, i in which:
            part = pl.ds(q * QUAD + i, STEP)
            chunk[q, i] = (to_right if q in (0, 3) else to_left)(e_v.at[part], ex_v.at[part])

    loads[0].wait()
    pl.semaphore_wait(barrier, owners - 1 + has_left.astype(jnp.int32) + has_right.astype(jnp.int32))
    send_chunks(order[:AHEAD])

    for cp in loads[1:5]:
        cp.wait()
    s_all, r_all = wide[0, 0:NF, :], wide[1, 0:NF, :]
    sums = []
    for q in range(4):

        def gather_energy(i, acc, q=q):
            d = q * QUAD + i
            e = e_v[d]
            return acc[0] + e, acc[1] + coef[d, 0] * e, acc[2] + coef[d, 1] * e

        zero = jnp.zeros((NF, 128), F32)
        sums.append(lax.fori_loop(0, QUAD, gather_energy, (zero, zero, zero), unroll=3))

    def over_f(x):
        return jnp.sum(x, axis=0, keepdims=True)

    gc = [x[1] for x in sums]
    gn = [x[2] for x in sums]
    en_xp, en_xm = over_f(s_all * (gc[0] + gc[3])), over_f(s_all * (gc[1] + gc[2]))
    en_yp, en_ym = over_f(s_all * (gn[0] + gn[1])), over_f(s_all * (gn[2] + gn[3]))
    en_own = over_f(sums[0][0] + sums[1][0] + sums[2][0] + sums[3][0]) - (en_xp + en_xm + en_yp + en_ym)
    en_yp, en_ym = pltpu.roll(en_yp, 1, 1), pltpu.roll(en_ym, 127, 1)

    w0, w1 = wind[0], wind[1]
    row8 = lax.broadcasted_iota(jnp.int32, (8, 128), 0)

    def tile(energy):
        return jnp.where(row8 == 0, energy, jnp.where(row8 == 1, w0, w1))

    xs[0], xs[1] = tile(en_xp), tile(en_xm)

    for side, last in ((0, 127), (1, 0)):
        pickup = jnp.where(lax.broadcasted_iota(jnp.int32, (16, 128), 1) == last, 1.0, 0.0).astype(BF16)
        high, low = split(flat_v[pl.ds(side * EDGE, EDGE), :])
        turned = (((1,), (1,)), ((), ()))
        ys[side, :, 0:128] = tile(en_yp if side == 0 else en_ym)
        ys[side, :, 128 : 128 + EDGE] = (mxu(pickup, high, turned) + mxu(pickup, low, turned))[0:8]
        ys[side, :, 128 + EDGE : 896] = jnp.zeros((8, 768 - EDGE), F32)
    early = [to_right(xs.at[0], xr.at[0]), to_left(xs.at[1], xr.at[1])]
    early += [to_up(ys.at[0], yr.at[0]), to_down(ys.at[1], yr.at[1])]

    send_chunks(order[AHEAD:])
    for cp in loads[5:]:
        cp.wait()

    lane8 = lax.broadcasted_iota(jnp.int32, (1, owners), 1)
    point = lax.broadcasted_iota(jnp.int32, (128, 128), 0)
    slot = lax.rem(lane, CAP)
    for j in range(owners):
        to = lax.rem(o + j, owners)
        picked = rows[pl.ds(to, 1), :]
        number = jnp.sum(jnp.where(lane8 == to, count[...], 0).astype(F32), axis=1, keepdims=True).astype(jnp.int32)
        hit = jnp.concatenate([picked, picked], axis=1) == point
        at = pl.ds(j * 128, 128)
        all_slots[:, at] = jnp.where(hit, 1.0, 0.0).astype(BF16)
        live_slots[:, at] = jnp.where(jnp.logical_and(hit, slot < number), 1.0, 0.0).astype(BF16)

    for j in range(owners):
        source = lax.rem(o + owners - j, owners)
        slots = lax.broadcasted_iota(jnp.int32, (CAP, opts), 0) + source * CAP
        total = jnp.zeros((CAP, opts), F32)
        for k in range(4):
            total = total + jnp.where(pick[k : k + 1, :] == slots, weight[k : k + 1, :], 0.0)
        high, low = split(total)
        m2[pl.ds(j * 128, CAP), :] = high
        m2[pl.ds(j * 128 + CAP, CAP), :] = low

    for arrive, _ in early:
        arrive()
    ct, nt = wide[2, 0:NF, :], wide[3, 0:NF, :]

    def driving(a, b):
        return 0.1 * jnp.maximum(a * ct + b * nt, 0.0)

    drive[0] = driving(w0, w1)
    drive[1] = jnp.where(
        ct > 0, driving(xr[1, 1:2, :], xr[1, 2:3, :]), driving(xr[0, 1:2, :], xr[0, 2:3, :])
    )
    up0 = jnp.where(lane == 127, pltpu.roll(yr[1, 1:2, 0:128], 127, 1), pltpu.roll(w0, 127, 1))
    up1 = jnp.where(lane == 127, pltpu.roll(yr[1, 2:3, 0:128], 127, 1), pltpu.roll(w1, 127, 1))
    dn0 = jnp.where(lane == 0, pltpu.roll(yr[0, 1:2, 0:128], 1, 1), pltpu.roll(w0, 1, 1))
    dn1 = jnp.where(lane == 0, pltpu.roll(yr[0, 2:3, 0:128], 1, 1), pltpu.roll(w1, 1, 1))
    drive[2] = jnp.where(nt > 0, driving(up0, up1), driving(dn0, dn1))
    energy = (
        en_own
        + xr[0, 0:1, :]
        + xr[1, 0:1, :]
        + jnp.where(lane == 0, down_in * yr[0, 0:1, 0:128], en_yp)
        + jnp.where(lane == 127, up_in * yr[1, 0:1, 0:128], en_ym)
    ) * (1.0 / (ND * NF))
    damp = 0.3 * (energy / (energy + 1.0))

    for side, (last, inside, shift) in enumerate(((0, down_in, 1), (127, up_in, 127))):
        place = jnp.where(lax.broadcasted_iota(jnp.int32, (16, 128), 1) == last, 1.0, 0.0)
        place = jnp.where(lax.rem(lax.broadcasted_iota(jnp.int32, (16, 128), 0), 8) == 0, place, 0.0).astype(BF16)
        high, low = split(yr[side, :, 128 : 128 + EDGE] * inside)
        both = jnp.concatenate([high.astype(F32), low.astype(F32)], axis=0).astype(BF16)
        edge_v[side] = mxu(both, place, (((0,), (0,)), ((), ())))
        for half in (0, 1):
            for i in range(QUAD):
                d = side * 2 * QUAD + half * QUAD + i
                e = e_v[d]
                k = (half * QUAD + i) * NF
                behind = jnp.where(lane == last, edge_v[side, k : k + NF, :], pltpu.roll(e, shift, 1))
                m_v[d] = e + s_all * (coef[d, 1] * behind - coef[d, 8] * e)

    carried = current[...]
    ones = jnp.ones((1, opts), F32)
    c_high = carried.astype(BF16).astype(F32)
    none = jnp.zeros((5, opts), F32)
    car = jnp.concatenate([c_high, ones, none, carried - c_high, jnp.zeros((6, opts), F32)], axis=0).astype(BF16)
    t = mxu(car, m2[...], (((1,), (1,)), ((), ())))
    t = t[0:8] + t[8:16]
    for j in range(owners):
        part = t[:, j * 128 : j * 128 + 128]
        ts[j] = part + pltpu.roll(part, CAP, 1)
    returns = {j: send(ts.at[j], tr.at[j], peer(owners - j)) for j in far_first}

    sea = mask[...].astype(F32)
    s_pad, r_pad = wide[0], wide[1]

    def contract(table, x):
        high, low = split(x)
        both = table[...].astype(BF16)
        out = mxu(both, high)
        return out[0:80] + out[80:160] + mxu(both[0:80], low)

    def finish(value, energy_row):
        tail = value[32:40] + jnp.where(row8 == 2, energy_row, 0.0)
        return (sea * jnp.concatenate([value[0:32], tail, value[40:80]], axis=0))[0:ROWS]

    def columns(acc_v, side):
        sums = [acc_v[side, g] for g in range(7)]
        parts = sums[1:5] + [sums[3] + r_pad * sums[5], sums[4] + r_pad * sums[6], jnp.zeros((16, 128), F32)]
        return jnp.concatenate(parts, axis=0), over_f(s_pad * sums[0])

    def advance(q, first):
        chunk[q, first][0]()
        x_side, y_side = (0 if q in (0, 3) else 1), (0 if q in (0, 1) else 1)
        for low, n in HALVES:
            part = pl.ds(low, n)
            r, s = wide[1, part, :], wide[0, part, :]
            acc = [ref[side, g, part, :] for ref, side in ((ax_v, x_side), (ay_v, y_side)) for g in range(7)]
            for i in range(STEP):
                d = q * QUAD + first + i
                moved = m_v[d, part, :] + s * (coef[d, 0] * ex_v[d, part, :])
                e = moved + moved * (r * (drive[0, d : d + 1, :] - damp))
                m_v[d, part, :] = e
                out = []
                for at, (a, kc, kn) in ((1, (0, 2, 3)), (2, (1, 4, 5))):
                    here = drive[at, d : d + 1, :]
                    e1 = e * here
                    e2 = e1 * here
                    a, kc, kn = coef[d, a], coef[d, kc], coef[d, kn]
                    out += [a * e, kc * e, kn * e, kc * e1, kn * e1, kc * e2, kn * e2]
                acc = [x + y for x, y in zip(acc, out)]
            for ref, side, values in ((ax_v, x_side, acc[:7]), (ay_v, y_side, acc[7:])):
                for g, value in enumerate(values):
                    ref[side, g, part, :] = value

    for q, first in order:
        advance(q, first)
    sides = [columns(ref, side) for ref in (ax_v, ay_v) for side in (0, 1)]
    out = contract(wxy, jnp.concatenate([x for x, _ in sides], axis=1))
    sums_out = []
    for at, (towards, shift) in enumerate(((to_right, 0), (to_left, 0), (to_up, 1), (to_down, 127))):
        value = finish(out[:, at * 128 : at * 128 + 128], sides[at][1])
        ps[at] = pltpu.roll(value, shift, 1) if shift else value
        sums_out.append(towards(ps.at[at], pr.at[at]))

    e_own = []
    for low, n in HALVES:
        part = pl.ds(low, n)
        r, s = wide[1, part, :], wide[0, part, :]

        def own_bins(d, acc, part=part, s=s):
            e = m_v[d, part, :]
            e = e - s * (coef[d, 8] * e)
            here = drive[0, pl.ds(d, 1), :]
            e1 = e * here
            e2 = e1 * here
            kc, kn = coef[d, 6], coef[d, 7]
            out = (e, kc * e, kn * e, kc * e1, kn * e1, kc * e2, kn * e2)
            return tuple(x + y for x, y in zip(acc, out))

        a = lax.fori_loop(0, ND, own_bins, (jnp.zeros((n, 128), F32),) * 7, unroll=4)
        for g, value in enumerate([a[1], a[2], a[3], a[4], a[3] + r * a[5], a[4] + r * a[6]]):
            oq[pl.ds(g * FP + low, n), :] = value
        e_own.append(over_f(a[0]))
    total = finish(contract(wown, oq[...]), e_own[0] + e_own[1])

    for j in range(1, owners):
        returns[j][0]()
    sums = []
    for j in range(owners):
        value = tr[j] if j else ts[0]
        high = value.astype(BF16).astype(F32)
        sums.append(jnp.where(lane < CAP, high, value - high))
    sums = jnp.concatenate(sums, axis=1)
    sums = jnp.concatenate([sums, jnp.zeros(sums.shape, F32)], axis=0).astype(BF16)
    got = mxu(sums, all_slots[...], (((1,), (1,)), ((), ())))
    back[:, 0, :] = got[0:2] / jnp.maximum(got[2:3], 1.0)

    for arrive, _ in sums_out:
        arrive()
    total = (
        total
        + pr[0]
        + pr[1]
        + jnp.where(lane == 0, down_in * pr[2], ps[2])
        + jnp.where(lane == 127, up_in * pr[3], ps[3])
    )
    energy = total[34:35] * (1.0 / (ND * NF))
    value = sea * (total[0:CH] - (energy / (energy + 1.0)) * total[40:ROWS])

    half = CH // 2
    gap = jnp.zeros((24 - half, 128), F32)

    def two_parts(x):
        high = x.astype(BF16).astype(F32)
        return jnp.concatenate([high, x - high], axis=0).astype(BF16)

    out = mxu(two_parts(jnp.concatenate([value[0:half], gap, value[half:CH], gap], axis=0)), live_slots[...])
    out = out[0:48] + out[48:96]
    fields = {}
    for j in far_first + [0]:
        at = slice(j * 128, j * 128 + 128)
        fs[j] = jnp.where(lane < CAP, out[0:half, at], out[24 : 24 + half, at])
        if j:
            fields[j] = send(fs.at[j], fr.at[j], peer(j))

    acc = jnp.zeros((96, opts), F32)
    for j in range(0, owners, 2):
        sides = []
        for k in (j, j + 1):
            if k:
                fields[k][0]()
            value = jnp.concatenate([fr[k] if k else fs[0], gap], axis=0)
            other = pltpu.roll(value, CAP, 1)
            sides.append(two_parts(jnp.concatenate([jnp.where(lane < CAP, value, other), jnp.where(lane < CAP, other, value)], axis=0)))
        acc = acc + mxu(jnp.concatenate(sides, axis=1), m2[j * 128 : j * 128 + 256, :])
    acc = acc[0:48] + acc[48:96]
    forcing[0:half, :] = acc[0:half]
    forcing[half:CH, :] = acc[24 : 24 + half]

    for _, leave in (*early, *chunk.values(), *returns.values(), *sums_out, *fields.values()):
        leave()


def write_out(forcing, back, forcing_hbm, back_hbm, sem):
    copies = [pltpu.make_async_copy(forcing, forcing_hbm, sem.at[0]), pltpu.make_async_copy(back, back_hbm, sem.at[1])]
    for cp in copies:
        cp.start()
    for cp in copies:
        cp.wait()


def per_device(spectra, surface_wind, water_mask, send_rows, send_count, pick_slot, pick_weight, ocean_current):
    strips, owners = lax.axis_size("wave"), lax.axis_size("ocean")
    opts = pick_slot.shape[1]
    coef, wide, wown, wxy = (jnp.asarray(x) for x in constants())
    anywhere = pl.BlockSpec(memory_space=pltpu.HBM)
    copies = 8 + ND // STEP + 2 * (owners - 1)

    def f32(*shape):
        return pltpu.VMEM(shape, F32)

    def i32(*shape):
        return pltpu.VMEM(shape, jnp.int32)

    results = pl.pallas_call(
        functools.partial(interval, strips, owners, opts),
        name="interval",
        out_shape=(
            jax.ShapeDtypeStruct((34, opts), F32),
            jax.ShapeDtypeStruct((2, 1, 128), F32),
        ),
        in_specs=[anywhere] * 13,
        out_specs=(pl.BlockSpec(memory_space=pltpu.VMEM),) * 2,
        scratch_shapes=[
            pltpu.SMEM((ND, 16), F32),
            f32(ND, NF, 128),
            f32(ND, NF, 128),
            f32(ND, NF, 128),
            f32(ND * NF, 128),
            f32(2, EDGE, 128),
            f32(2, 1, 128),
            i32(1, 128),
            i32(owners, CAP),
            i32(1, owners),
            i32(4, opts),
            f32(4, opts),
            f32(2, opts),
            f32(4, FP, 128),
            f32(160, 256),
            f32(160, 256),
            f32(3, NF, 128),
            f32(2, 7, FP, 128),
            f32(2, 7, FP, 128),
            f32(256, 128),
            f32(2, 8, 128),
            f32(2, 8, 128),
            f32(2, 8, 896),
            f32(2, 8, 896),
            f32(4, ROWS, 128),
            f32(4, ROWS, 128),
            f32(owners, CH // 2, 128),
            f32(owners, CH // 2, 128),
            f32(owners, 8, 128),
            f32(owners, 8, 128),
            pltpu.VMEM((owners * 128, opts), BF16),
            pltpu.VMEM((128, owners * 128), BF16),
            pltpu.VMEM((128, owners * 128), BF16),
            pltpu.SemaphoreType.DMA((13,)),
            pltpu.SemaphoreType.DMA((copies,)),
            pltpu.SemaphoreType.DMA((copies,)),
        ],
        compiler_params=pltpu.CompilerParams(collective_id=0, has_side_effects=True, vmem_limit_bytes=32 << 20),
    )(
        *(
            pltpu.with_memory_space_constraint(x, pltpu.HBM)
            for x in (
                coef,
                spectra.reshape(ND, NF, 1, 128),
                spectra.reshape(ND * NF, 128),
                surface_wind,
                water_mask,
                send_rows,
                send_count.reshape(1, owners),
                pick_slot,
                pick_weight,
                ocean_current,
                wide,
                wown,
                wxy,
            )
        )
    )
    return pl.pallas_call(
        write_out,
        name="write_out",
        out_shape=(
            jax.ShapeDtypeStruct((34, opts), F32),
            jax.ShapeDtypeStruct((2, 1, 128), F32),
        ),
        in_specs=[pl.BlockSpec(memory_space=pltpu.VMEM)] * 2,
        out_specs=(anywhere,) * 2,
        scratch_shapes=[pltpu.SemaphoreType.DMA((2,))],
    )(*(pltpu.with_memory_space_constraint(x, pltpu.VMEM) for x in results))


def solution(mesh):
    in_specs = (
        P("wave", None, None, "ocean"),
        P(None, "wave", "ocean"),
        P("wave", "ocean"),
        P(None, ("wave", "ocean")),
        P(None, ("wave", "ocean")),
        P(None, ("wave", "ocean")),
        P(None, ("wave", "ocean")),
        P(None, ("wave", "ocean")),
    )
    out_specs = (P(None, ("wave", "ocean")), P(None, "wave", "ocean"))
    return jax.shard_map(per_device, mesh=mesh, in_specs=in_specs, out_specs=out_specs, check_vma=False)
```

```python
import functools

import jax
import jax.numpy as jnp
import ml_dtypes
import numpy as np
from jax import lax
from jax.experimental import pallas as pl
from jax.experimental.pallas import tpu as pltpu
from jax.sharding import PartitionSpec as P

ND = 36
NF = 36
FP = 40
DEPTHS = 16
CAP = 64
QUAD = 9
MESH = pl.DeviceIdType.MESH
F32 = jnp.float32
BF16 = jnp.bfloat16
HALVES = ((0, 16), (16, 20))
STEP = 3
AHEAD = 4
ROWS = 74
CH = 34
EDGE = QUAD * 2 * NF


def host_tables():
    angles = (np.arange(ND) + 0.5) * (2.0 * np.pi / ND)
    cosine, sines = np.cos(angles), np.sin(angles)
    frequency = np.arange(NF)
    speeds = 0.7 * 1.1 ** (-frequency)
    ratios = 1.1 ** (frequency - (NF - 1.0))
    kappas = 0.02 * 1.1 ** (2.0 * frequency)
    depths = 0.25 * np.arange(DEPTHS)
    kernel = np.sqrt(kappas)[:, None] * np.exp(-2.0 * kappas[:, None] * depths[None, :])
    return cosine, sines, speeds, ratios, kernel


def split_rows(values):
    high = values.astype(ml_dtypes.bfloat16)
    low = (values - high.astype(np.float64)).astype(ml_dtypes.bfloat16)
    return np.concatenate([high, low], 0).astype(np.float32)


def projection(scale):
    _, _, _, ratios, kernel = host_tables()
    table = np.zeros((80, 256))

    def put(row, group, values):
        table[row, group * FP : group * FP + NF] = values * scale / ND

    for depth in range(DEPTHS):
        k = kernel[:, depth]
        for side in (0, 1):
            put(16 * side + depth, side, k)
            put(16 * side + depth, 2 + side, k * ratios)
            put(40 + 16 * side + depth, side, 0.3 * k * ratios)
    for side in (0, 1):
        put(32 + side, 4 + side, ratios)
        put(72 + side, 2 + side, 0.3 * ratios * ratios)
    return split_rows(table)


def constants():
    cosine, sines, speeds, ratios, _ = host_tables()
    ac, an = np.abs(cosine), np.abs(sines)
    coef = np.zeros((ND, 16))
    for i, column in enumerate((ac, an, cosine * ac, sines * ac, cosine * an, sines * an, cosine, sines, ac + an)):
        coef[:, i] = column
    wide = np.zeros((4, FP, 128))
    for i, column in enumerate((speeds, ratios, cosine, sines)):
        wide[i, :36] = column[:, None]
    return (
        coef.astype(np.float32),
        wide.astype(np.float32),
        projection(np.ones(NF)),
        projection(speeds),
    )


def mxu(a, b, dims=(((1,), (0,)), ((), ()))):
    return lax.dot_general(a, b, dims, preferred_element_type=F32)


def split(x):
    high = x.astype(BF16)
    return high, (x - high.astype(F32)).astype(BF16)


def interval(
    strips,
    owners,
    opts,
    coef_hbm,
    spectra,
    flat,
    wind_hbm,
    mask_hbm,
    rows_hbm,
    count_hbm,
    pick_hbm,
    weight_hbm,
    current_hbm,
    wide_hbm,
    wown_hbm,
    wxy_hbm,
    forcing,
    back,
    coef,
    e_v,
    ex_v,
    m_v,
    flat_v,
    edge_v,
    wind,
    mask,
    rows,
    count,
    pick,
    weight,
    current,
    wide,
    wown,
    wxy,
    drive,
    ax_v,
    ay_v,
    oq,
    xs,
    xr,
    ys,
    yr,
    ps,
    pr,
    fs,
    fr,
    ts,
    tr,
    m2,
    all_slots,
    live_slots,
    local_sem,
    send_sem,
    recv_sem,
    word_sem,
):
    w, o = lax.axis_index("wave"), lax.axis_index("ocean")
    xp, xm = (lax.rem(w + 1, strips), o), (lax.rem(w + strips - 1, strips), o)
    yp, ym = (w, lax.rem(o + 1, owners)), (w, lax.rem(o + owners - 1, owners))

    def peer(j):
        return (w, lax.rem(o + j, owners))

    far_first = sorted(range(1, owners), key=lambda j: -min(j, owners - j))

    has_left, has_right = w > 0, w < strips - 1

    barrier = pltpu.get_barrier_semaphore()

    def greet(device):
        pl.semaphore_signal(barrier, inc=1, device_id=device, device_id_type=MESH)

    pl.when(has_right)(lambda: greet(xp))
    pl.when(has_left)(lambda: greet(xm))
    greet(yp)
    greet(ym)

    loads = []
    for src, dst in (
        (spectra.at[:, :, 0, :], e_v),
        (coef_hbm, coef),
        (wind_hbm, wind),
        (wide_hbm, wide),
        (flat, flat_v),
        (rows_hbm, rows),
        (count_hbm, count),
        (mask_hbm, mask),
        (pick_hbm, pick),
        (weight_hbm, weight),
        (current_hbm, current),
        (wxy_hbm, wxy),
        (wown_hbm, wown),
    ):
        cp = pltpu.make_async_copy(src, dst, local_sem.at[len(loads)])
        cp.start()
        loads.append(cp)

    used = [0]

    def send(src, dst, device, there=None, back=None):
        i = used[0]
        used[0] += 1
        cp = pltpu.make_async_remote_copy(
            src_ref=src, dst_ref=dst, send_sem=send_sem.at[i], recv_sem=recv_sem.at[i], device_id=device, device_id_type=MESH
        )

        def under(condition, action):
            if condition is None:
                action()
            else:
                pl.when(condition)(action)

        under(there, cp.start)
        return lambda: under(back, cp.wait_recv), lambda: under(there, cp.wait_send)

    def to_right(src, dst):
        return send(src, dst, xp, has_right, has_left)

    def to_left(src, dst):
        return send(src, dst, xm, has_left, has_right)

    def to_up(src, dst):
        return send(src, dst, yp)

    def to_down(src, dst):
        return send(src, dst, ym)

    down_in = jnp.where(o > 0, 1.0, 0.0).astype(F32)
    up_in = jnp.where(o < owners - 1, 1.0, 0.0).astype(F32)
    lane = lax.broadcasted_iota(jnp.int32, (1, 128), 1)

    oq[...] = jnp.zeros(oq.shape, F32)
    ax_v[...] = jnp.zeros(ax_v.shape, F32)
    ay_v[...] = jnp.zeros(ay_v.shape, F32)

    @pl.when(jnp.logical_not(has_left))
    def _():
        ex_v[0:QUAD] = jnp.zeros((QUAD, NF, 128), F32)
        ex_v[3 * QUAD : ND] = jnp.zeros((QUAD, NF, 128), F32)
        xr[0] = jnp.zeros((8, 128), F32)
        pr[0] = jnp.zeros((ROWS, 128), F32)

    @pl.when(jnp.logical_not(has_right))
    def _():
        ex_v[QUAD : 3 * QUAD] = jnp.zeros((2 * QUAD, NF, 128), F32)
        xr[1] = jnp.zeros((8, 128), F32)
        pr[1] = jnp.zeros((ROWS, 128), F32)

    order = [(q, i) for pair in ((0, 2), (3, 1)) for i in range(0, QUAD, STEP) for q in pair]
    chunk = {}

    def send_chunks(which):
        for q, i in which:
            part = pl.ds(q * QUAD + i, STEP)
            chunk[q, i] = (to_right if q in (0, 3) else to_left)(e_v.at[part], ex_v.at[part])

    loads[0].wait()
    pl.semaphore_wait(barrier, 2 + has_left.astype(jnp.int32) + has_right.astype(jnp.int32))
    send_chunks(order[:AHEAD])

    rounds = (owners - 2 + 1) // 2

    def tell(r):
        if r < rounds:
            pl.semaphore_signal(word_sem.at[r, 0], inc=1, device_id=yp, device_id_type=MESH)
            pl.semaphore_signal(word_sem.at[r, 1], inc=1, device_id=ym, device_id_type=MESH)

    def hear(r):
        if r < rounds:
            pl.semaphore_wait(word_sem.at[r, 0], 1)
            pl.semaphore_wait(word_sem.at[r, 1], 1)
            tell(r + 1)

    tell(0)

    for cp in loads[1:5]:
        cp.wait()
    s_all, r_all = wide[0, 0:NF, :], wide[1, 0:NF, :]
    sums = []
    for q in range(4):

        def gather_energy(i, acc, q=q):
            d = q * QUAD + i
            e = e_v[d]
            return acc[0] + e, acc[1] + coef[d, 0] * e, acc[2] + coef[d, 1] * e

        zero = jnp.zeros((NF, 128), F32)
        sums.append(lax.fori_loop(0, QUAD, gather_energy, (zero, zero, zero), unroll=3))

    def over_f(x):
        return jnp.sum(x, axis=0, keepdims=True)

    gc = [x[1] for x in sums]
    gn = [x[2] for x in sums]
    en_xp, en_xm = over_f(s_all * (gc[0] + gc[3])), over_f(s_all * (gc[1] + gc[2]))
    en_yp, en_ym = over_f(s_all * (gn[0] + gn[1])), over_f(s_all * (gn[2] + gn[3]))
    en_own = over_f(sums[0][0] + sums[1][0] + sums[2][0] + sums[3][0]) - (en_xp + en_xm + en_yp + en_ym)
    en_yp, en_ym = pltpu.roll(en_yp, 1, 1), pltpu.roll(en_ym, 127, 1)

    w0, w1 = wind[0], wind[1]
    row8 = lax.broadcasted_iota(jnp.int32, (8, 128), 0)

    def tile(energy):
        return jnp.where(row8 == 0, energy, jnp.where(row8 == 1, w0, w1))

    xs[0], xs[1] = tile(en_xp), tile(en_xm)

    for side, last in ((0, 127), (1, 0)):
        pickup = jnp.where(lax.broadcasted_iota(jnp.int32, (16, 128), 1) == last, 1.0, 0.0).astype(BF16)
        high, low = split(flat_v[pl.ds(side * EDGE, EDGE), :])
        turned = (((1,), (1,)), ((), ()))
        ys[side, :, 0:128] = tile(en_yp if side == 0 else en_ym)
        ys[side, :, 128 : 128 + EDGE] = (mxu(pickup, high, turned) + mxu(pickup, low, turned))[0:8]
        ys[side, :, 128 + EDGE : 896] = jnp.zeros((8, 768 - EDGE), F32)
    early = [to_right(xs.at[0], xr.at[0]), to_left(xs.at[1], xr.at[1])]
    early += [to_up(ys.at[0], yr.at[0]), to_down(ys.at[1], yr.at[1])]

    send_chunks(order[AHEAD:])
    for cp in loads[5:]:
        cp.wait()

    hear(0)

    lane8 = lax.broadcasted_iota(jnp.int32, (1, owners), 1)
    point = lax.broadcasted_iota(jnp.int32, (128, 128), 0)
    slot = lax.rem(lane, CAP)
    for j in range(owners):
        to = lax.rem(o + j, owners)
        picked = rows[pl.ds(to, 1), :]
        number = jnp.sum(jnp.where(lane8 == to, count[...], 0).astype(F32), axis=1, keepdims=True).astype(jnp.int32)
        hit = jnp.concatenate([picked, picked], axis=1) == point
        at = pl.ds(j * 128, 128)
        all_slots[:, at] = jnp.where(hit, 1.0, 0.0).astype(BF16)
        live_slots[:, at] = jnp.where(jnp.logical_and(hit, slot < number), 1.0, 0.0).astype(BF16)

    hear(1)

    for j in range(owners):
        source = lax.rem(o + owners - j, owners)
        slots = lax.broadcasted_iota(jnp.int32, (CAP, opts), 0) + source * CAP
        total = jnp.zeros((CAP, opts), F32)
        for k in range(4):
            total = total + jnp.where(pick[k : k + 1, :] == slots, weight[k : k + 1, :], 0.0)
        high, low = split(total)
        m2[pl.ds(j * 128, CAP), :] = high
        m2[pl.ds(j * 128 + CAP, CAP), :] = low

    carried = current[...]
    ones = jnp.ones((1, opts), F32)
    c_high = carried.astype(BF16).astype(F32)
    none = jnp.zeros((5, opts), F32)
    car = jnp.concatenate([c_high, ones, none, carried - c_high, jnp.zeros((6, opts), F32)], axis=0).astype(BF16)
    t = mxu(car, m2[...], (((1,), (1,)), ((), ())))
    t = t[0:8] + t[8:16]
    for j in range(owners):
        part = t[:, j * 128 : j * 128 + 128]
        ts[j] = part + pltpu.roll(part, CAP, 1)
    for r in range(2, rounds):
        hear(r)
    returns = {j: send(ts.at[j], tr.at[j], peer(owners - j)) for j in far_first}

    for arrive, _ in early:
        arrive()
    ct, nt = wide[2, 0:NF, :], wide[3, 0:NF, :]

    def driving(a, b):
        return 0.1 * jnp.maximum(a * ct + b * nt, 0.0)

    drive[0] = driving(w0, w1)
    drive[1] = jnp.where(
        ct > 0, driving(xr[1, 1:2, :], xr[1, 2:3, :]), driving(xr[0, 1:2, :], xr[0, 2:3, :])
    )
    up0 = jnp.where(lane == 127, pltpu.roll(yr[1, 1:2, 0:128], 127, 1), pltpu.roll(w0, 127, 1))
    up1 = jnp.where(lane == 127, pltpu.roll(yr[1, 2:3, 0:128], 127, 1), pltpu.roll(w1, 127, 1))
    dn0 = jnp.where(lane == 0, pltpu.roll(yr[0, 1:2, 0:128], 1, 1), pltpu.roll(w0, 1, 1))
    dn1 = jnp.where(lane == 0, pltpu.roll(yr[0, 2:3, 0:128], 1, 1), pltpu.roll(w1, 1, 1))
    drive[2] = jnp.where(nt > 0, driving(up0, up1), driving(dn0, dn1))
    energy = (
        en_own
        + xr[0, 0:1, :]
        + xr[1, 0:1, :]
        + jnp.where(lane == 0, down_in * yr[0, 0:1, 0:128], en_yp)
        + jnp.where(lane == 127, up_in * yr[1, 0:1, 0:128], en_ym)
    ) * (1.0 / (ND * NF))
    damp = 0.3 * (energy / (energy + 1.0))

    for side, (last, inside, shift) in enumerate(((0, down_in, 1), (127, up_in, 127))):
        place = jnp.where(lax.broadcasted_iota(jnp.int32, (16, 128), 1) == last, 1.0, 0.0)
        place = jnp.where(lax.rem(lax.broadcasted_iota(jnp.int32, (16, 128), 0), 8) == 0, place, 0.0).astype(BF16)
        high, low = split(yr[side, :, 128 : 128 + EDGE] * inside)
        both = jnp.concatenate([high.astype(F32), low.astype(F32)], axis=0).astype(BF16)
        edge_v[side] = mxu(both, place, (((0,), (0,)), ((), ())))
        for half in (0, 1):
            for i in range(QUAD):
                d = side * 2 * QUAD + half * QUAD + i
                e = e_v[d]
                k = (half * QUAD + i) * NF
                behind = jnp.where(lane == last, edge_v[side, k : k + NF, :], pltpu.roll(e, shift, 1))
                m_v[d] = e + s_all * (coef[d, 1] * behind - coef[d, 8] * e)

    sea = mask[...].astype(F32)
    s_pad, r_pad = wide[0], wide[1]

    def contract(table, x):
        high, low = split(x)
        both = table[...].astype(BF16)
        out = mxu(both, high)
        return out[0:80] + out[80:160] + mxu(both[0:80], low)

    def finish(value, energy_row):
        tail = value[32:40] + jnp.where(row8 == 2, energy_row, 0.0)
        return (sea * jnp.concatenate([value[0:32], tail, value[40:80]], axis=0))[0:ROWS]

    def columns(acc_v, side):
        sums = [acc_v[side, g] for g in range(7)]
        parts = sums[1:5] + [sums[3] + r_pad * sums[5], sums[4] + r_pad * sums[6], jnp.zeros((16, 128), F32)]
        return jnp.concatenate(parts, axis=0), over_f(s_pad * sums[0])

    def advance(q, first):
        chunk[q, first][0]()
        x_side, y_side = (0 if q in (0, 3) else 1), (0 if q in (0, 1) else 1)
        for low, n in HALVES:
            part = pl.ds(low, n)
            r, s = wide[1, part, :], wide[0, part, :]
            acc = [ref[side, g, part, :] for ref, side in ((ax_v, x_side), (ay_v, y_side)) for g in range(7)]
            for i in range(STEP):
                d = q * QUAD + first + i
                moved = m_v[d, part, :] + s * (coef[d, 0] * ex_v[d, part, :])
                e = moved + moved * (r * (drive[0, d : d + 1, :] - damp))
                m_v[d, part, :] = e
                out = []
                for at, (a, kc, kn) in ((1, (0, 2, 3)), (2, (1, 4, 5))):
                    here = drive[at, d : d + 1, :]
                    e1 = e * here
                    e2 = e1 * here
                    a, kc, kn = coef[d, a], coef[d, kc], coef[d, kn]
                    out += [a * e, kc * e, kn * e, kc * e1, kn * e1, kc * e2, kn * e2]
                acc = [x + y for x, y in zip(acc, out)]
            for ref, side, values in ((ax_v, x_side, acc[:7]), (ay_v, y_side, acc[7:])):
                for g, value in enumerate(values):
                    ref[side, g, part, :] = value

    for q, first in order:
        if q in (0, 3):
            advance(q, first)
    sums_out = []

    def project(picks):
        sides = [columns(ref, side) for ref, side, _, _ in picks]
        out = contract(wxy, jnp.concatenate([x for x, _ in sides], axis=1))
        for i, (ref, side, towards, shift) in enumerate(picks):
            at = len(sums_out)
            value = finish(out[:, i * 128 : i * 128 + 128], sides[i][1])
            ps[at] = pltpu.roll(value, shift, 1) if shift else value
            sums_out.append(towards(ps.at[at], pr.at[at]))

    project([(ax_v, 0, to_right, 0)])
    for q, first in order:
        if q in (2, 1):
            advance(q, first)
    project([(ax_v, 1, to_left, 0), (ay_v, 0, to_up, 1), (ay_v, 1, to_down, 127)])

    e_own = []
    for low, n in HALVES:
        part = pl.ds(low, n)
        r, s = wide[1, part, :], wide[0, part, :]

        def own_bins(d, acc, part=part, s=s):
            e = m_v[d, part, :]
            e = e - s * (coef[d, 8] * e)
            here = drive[0, pl.ds(d, 1), :]
            e1 = e * here
            e2 = e1 * here
            kc, kn = coef[d, 6], coef[d, 7]
            out = (e, kc * e, kn * e, kc * e1, kn * e1, kc * e2, kn * e2)
            return tuple(x + y for x, y in zip(acc, out))

        a = lax.fori_loop(0, ND, own_bins, (jnp.zeros((n, 128), F32),) * 7, unroll=4)
        for g, value in enumerate([a[1], a[2], a[3], a[4], a[3] + r * a[5], a[4] + r * a[6]]):
            oq[pl.ds(g * FP + low, n), :] = value
        e_own.append(over_f(a[0]))
    total = finish(contract(wown, oq[...]), e_own[0] + e_own[1])

    for j in range(1, owners):
        returns[j][0]()
    sums = []
    for j in range(owners):
        value = tr[j] if j else ts[0]
        high = value.astype(BF16).astype(F32)
        sums.append(jnp.where(lane < CAP, high, value - high))
    sums = jnp.concatenate(sums, axis=1)
    sums = jnp.concatenate([sums, jnp.zeros(sums.shape, F32)], axis=0).astype(BF16)
    got = mxu(sums, all_slots[...], (((1,), (1,)), ((), ())))
    back[:, 0, :] = got[0:2] / jnp.maximum(got[2:3], 1.0)

    for arrive, _ in sums_out:
        arrive()
    total = (
        total
        + pr[0]
        + pr[1]
        + jnp.where(lane == 0, down_in * pr[2], ps[2])
        + jnp.where(lane == 127, up_in * pr[3], ps[3])
    )
    energy = total[34:35] * (1.0 / (ND * NF))
    value = sea * (total[0:CH] - (energy / (energy + 1.0)) * total[40:ROWS])

    half = CH // 2
    gap = jnp.zeros((24 - half, 128), F32)

    def two_parts(x):
        high = x.astype(BF16).astype(F32)
        return jnp.concatenate([high, x - high], axis=0).astype(BF16)

    out = mxu(two_parts(jnp.concatenate([value[0:half], gap, value[half:CH], gap], axis=0)), live_slots[...])
    out = out[0:48] + out[48:96]
    fields = {}
    for j in far_first + [0]:
        at = slice(j * 128, j * 128 + 128)
        fs[j] = jnp.where(lane < CAP, out[0:half, at], out[24 : 24 + half, at])
        if j:
            fields[j] = send(fs.at[j], fr.at[j], peer(j))

    acc = jnp.zeros((96, opts), F32)
    for j in range(0, owners, 2):
        sides = []
        for k in (j, j + 1):
            if k:
                fields[k][0]()
            value = jnp.concatenate([fr[k] if k else fs[0], gap], axis=0)
            other = pltpu.roll(value, CAP, 1)
            sides.append(two_parts(jnp.concatenate([jnp.where(lane < CAP, value, other), jnp.where(lane < CAP, other, value)], axis=0)))
        acc = acc + mxu(jnp.concatenate(sides, axis=1), m2[j * 128 : j * 128 + 256, :])
    acc = acc[0:48] + acc[48:96]
    forcing[0:half, :] = acc[0:half]
    forcing[half:CH, :] = acc[24 : 24 + half]

    for _, leave in (*early, *chunk.values(), *returns.values(), *sums_out, *fields.values()):
        leave()


def write_out(forcing, back, forcing_hbm, back_hbm, sem):
    copies = [pltpu.make_async_copy(forcing, forcing_hbm, sem.at[0]), pltpu.make_async_copy(back, back_hbm, sem.at[1])]
    for cp in copies:
        cp.start()
    for cp in copies:
        cp.wait()


def per_device(spectra, surface_wind, water_mask, send_rows, send_count, pick_slot, pick_weight, ocean_current):
    strips, owners = lax.axis_size("wave"), lax.axis_size("ocean")
    opts = pick_slot.shape[1]
    coef, wide, wown, wxy = (jnp.asarray(x) for x in constants())
    anywhere = pl.BlockSpec(memory_space=pltpu.HBM)
    copies = 8 + ND // STEP + 2 * (owners - 1)

    def f32(*shape):
        return pltpu.VMEM(shape, F32)

    def i32(*shape):
        return pltpu.VMEM(shape, jnp.int32)

    results = pl.pallas_call(
        functools.partial(interval, strips, owners, opts),
        name="interval",
        out_shape=(
            jax.ShapeDtypeStruct((34, opts), F32),
            jax.ShapeDtypeStruct((2, 1, 128), F32),
        ),
        in_specs=[anywhere] * 13,
        out_specs=(pl.BlockSpec(memory_space=pltpu.VMEM),) * 2,
        scratch_shapes=[
            pltpu.SMEM((ND, 16), F32),
            f32(ND, NF, 128),
            f32(ND, NF, 128),
            f32(ND, NF, 128),
            f32(ND * NF, 128),
            f32(2, EDGE, 128),
            f32(2, 1, 128),
            i32(1, 128),
            i32(owners, CAP),
            i32(1, owners),
            i32(4, opts),
            f32(4, opts),
            f32(2, opts),
            f32(4, FP, 128),
            f32(160, 256),
            f32(160, 256),
            f32(3, NF, 128),
            f32(2, 7, FP, 128),
            f32(2, 7, FP, 128),
            f32(256, 128),
            f32(2, 8, 128),
            f32(2, 8, 128),
            f32(2, 8, 896),
            f32(2, 8, 896),
            f32(4, ROWS, 128),
            f32(4, ROWS, 128),
            f32(owners, CH // 2, 128),
            f32(owners, CH // 2, 128),
            f32(owners, 8, 128),
            f32(owners, 8, 128),
            pltpu.VMEM((owners * 128, opts), BF16),
            pltpu.VMEM((128, owners * 128), BF16),
            pltpu.VMEM((128, owners * 128), BF16),
            pltpu.SemaphoreType.DMA((13,)),
            pltpu.SemaphoreType.DMA((copies,)),
            pltpu.SemaphoreType.DMA((copies,)),
            pltpu.SemaphoreType.REGULAR((max((owners - 1) // 2, 1), 2)),
        ],
        compiler_params=pltpu.CompilerParams(collective_id=0, has_side_effects=True, vmem_limit_bytes=32 << 20),
    )(
        *(
            pltpu.with_memory_space_constraint(x, pltpu.HBM)
            for x in (
                coef,
                spectra.reshape(ND, NF, 1, 128),
                spectra.reshape(ND * NF, 128),
                surface_wind,
                water_mask,
                send_rows,
                send_count.reshape(1, owners),
                pick_slot,
                pick_weight,
                ocean_current,
                wide,
                wown,
                wxy,
            )
        )
    )
    return pl.pallas_call(
        write_out,
        name="write_out",
        out_shape=(
            jax.ShapeDtypeStruct((34, opts), F32),
            jax.ShapeDtypeStruct((2, 1, 128), F32),
        ),
        in_specs=[pl.BlockSpec(memory_space=pltpu.VMEM)] * 2,
        out_specs=(anywhere,) * 2,
        scratch_shapes=[pltpu.SemaphoreType.DMA((2,))],
    )(*(pltpu.with_memory_space_constraint(x, pltpu.VMEM) for x in results))


def solution(mesh):
    in_specs = (
        P("wave", None, None, "ocean"),
        P(None, "wave", "ocean"),
        P("wave", "ocean"),
        P(None, ("wave", "ocean")),
        P(None, ("wave", "ocean")),
        P(None, ("wave", "ocean")),
        P(None, ("wave", "ocean")),
        P(None, ("wave", "ocean")),
    )
    out_specs = (P(None, ("wave", "ocean")), P(None, "wave", "ocean"))
    return jax.shard_map(per_device, mesh=mesh, in_specs=in_specs, out_specs=out_specs, check_vma=False)
```

```python
import functools

import jax
import jax.numpy as jnp
import ml_dtypes
import numpy as np
from jax import lax
from jax.experimental import pallas as pl
from jax.experimental.pallas import tpu as pltpu
from jax.sharding import PartitionSpec as P

ND = 36
NF = 36
FP = 40
DEPTHS = 16
CAP = 64
QUAD = 9
MESH = pl.DeviceIdType.MESH
F32 = jnp.float32
BF16 = jnp.bfloat16
HALVES = ((0, 16), (16, 20))
STEP = 3
AHEAD = 4
ROWS = 74
CH = 34
EDGE = QUAD * 2 * NF


def host_tables():
    angles = (np.arange(ND) + 0.5) * (2.0 * np.pi / ND)
    cosine, sines = np.cos(angles), np.sin(angles)
    frequency = np.arange(NF)
    speeds = 0.7 * 1.1 ** (-frequency)
    ratios = 1.1 ** (frequency - (NF - 1.0))
    kappas = 0.02 * 1.1 ** (2.0 * frequency)
    depths = 0.25 * np.arange(DEPTHS)
    kernel = np.sqrt(kappas)[:, None] * np.exp(-2.0 * kappas[:, None] * depths[None, :])
    return cosine, sines, speeds, ratios, kernel


def split_rows(values):
    high = values.astype(ml_dtypes.bfloat16)
    low = (values - high.astype(np.float64)).astype(ml_dtypes.bfloat16)
    return np.concatenate([high, low], 0).astype(np.float32)


def projection(scale):
    _, _, _, ratios, kernel = host_tables()
    table = np.zeros((80, 256))

    def put(row, group, values):
        table[row, group * FP : group * FP + NF] = values * scale / ND

    for depth in range(DEPTHS):
        k = kernel[:, depth]
        for side in (0, 1):
            put(16 * side + depth, side, k)
            put(16 * side + depth, 2 + side, k * ratios)
            put(40 + 16 * side + depth, side, 0.3 * k * ratios)
    for side in (0, 1):
        put(32 + side, 4 + side, ratios)
        put(72 + side, 2 + side, 0.3 * ratios * ratios)
    return split_rows(table)


def constants():
    cosine, sines, speeds, ratios, _ = host_tables()
    ac, an = np.abs(cosine), np.abs(sines)
    coef = np.zeros((ND, 16))
    for i, column in enumerate((ac, an, cosine * ac, sines * ac, cosine * an, sines * an, cosine, sines, ac + an)):
        coef[:, i] = column
    wide = np.zeros((4, FP, 128))
    for i, column in enumerate((speeds, ratios, cosine, sines)):
        wide[i, :36] = column[:, None]
    return (
        coef.astype(np.float32),
        wide.astype(np.float32),
        projection(np.ones(NF)),
        projection(speeds),
    )


def mxu(a, b, dims=(((1,), (0,)), ((), ()))):
    return lax.dot_general(a, b, dims, preferred_element_type=F32)


def split(x):
    high = x.astype(BF16)
    return high, (x - high.astype(F32)).astype(BF16)


def interval(
    strips,
    owners,
    opts,
    coef_hbm,
    spectra,
    flat,
    wind_hbm,
    mask_hbm,
    rows_hbm,
    count_hbm,
    pick_hbm,
    weight_hbm,
    current_hbm,
    wide_hbm,
    wown_hbm,
    wxy_hbm,
    forcing,
    back,
    coef,
    e_v,
    ex_v,
    m_v,
    flat_v,
    edge_v,
    wind,
    mask,
    rows,
    count,
    pick,
    weight,
    current,
    wide,
    wown,
    wxy,
    drive,
    ax_v,
    ay_v,
    oq,
    xs,
    xr,
    ys,
    yr,
    ps,
    pr,
    fs,
    fr,
    ts,
    tr,
    m2,
    all_slots,
    live_slots,
    local_sem,
    send_sem,
    recv_sem,
    word_sem,
):
    w, o = lax.axis_index("wave"), lax.axis_index("ocean")
    xp, xm = (lax.rem(w + 1, strips), o), (lax.rem(w + strips - 1, strips), o)
    yp, ym = (w, lax.rem(o + 1, owners)), (w, lax.rem(o + owners - 1, owners))

    def peer(j):
        return (w, lax.rem(o + j, owners))

    far_first = sorted(range(1, owners), key=lambda j: -min(j, owners - j))

    has_left, has_right = w > 0, w < strips - 1

    barrier = pltpu.get_barrier_semaphore()

    def greet(device):
        pl.semaphore_signal(barrier, inc=1, device_id=device, device_id_type=MESH)

    pl.when(has_right)(lambda: greet(xp))
    pl.when(has_left)(lambda: greet(xm))
    greet(yp)
    greet(ym)

    loads = []
    for src, dst in (
        (spectra.at[:, :, 0, :], e_v),
        (coef_hbm, coef),
        (wind_hbm, wind),
        (wide_hbm, wide),
        (flat, flat_v),
        (rows_hbm, rows),
        (count_hbm, count),
        (mask_hbm, mask),
        (pick_hbm, pick),
        (weight_hbm, weight),
        (current_hbm, current),
        (wxy_hbm, wxy),
        (wown_hbm, wown),
    ):
        cp = pltpu.make_async_copy(src, dst, local_sem.at[len(loads)])
        cp.start()
        loads.append(cp)

    used = [0]

    def send(src, dst, device, there=None, back=None):
        i = used[0]
        used[0] += 1
        cp = pltpu.make_async_remote_copy(
            src_ref=src, dst_ref=dst, send_sem=send_sem.at[i], recv_sem=recv_sem.at[i], device_id=device, device_id_type=MESH
        )

        def under(condition, action):
            if condition is None:
                action()
            else:
                pl.when(condition)(action)

        under(there, cp.start)
        return lambda: under(back, cp.wait_recv), lambda: under(there, cp.wait_send)

    def to_right(src, dst):
        return send(src, dst, xp, has_right, has_left)

    def to_left(src, dst):
        return send(src, dst, xm, has_left, has_right)

    def to_up(src, dst):
        return send(src, dst, yp)

    def to_down(src, dst):
        return send(src, dst, ym)

    down_in = jnp.where(o > 0, 1.0, 0.0).astype(F32)
    up_in = jnp.where(o < owners - 1, 1.0, 0.0).astype(F32)
    lane = lax.broadcasted_iota(jnp.int32, (1, 128), 1)

    oq[...] = jnp.zeros(oq.shape, F32)
    ax_v[...] = jnp.zeros(ax_v.shape, F32)
    ay_v[...] = jnp.zeros(ay_v.shape, F32)

    @pl.when(jnp.logical_not(has_left))
    def _():
        ex_v[0:QUAD] = jnp.zeros((QUAD, NF, 128), F32)
        ex_v[3 * QUAD : ND] = jnp.zeros((QUAD, NF, 128), F32)
        xr[0] = jnp.zeros((8, 128), F32)
        pr[0] = jnp.zeros((ROWS, 128), F32)

    @pl.when(jnp.logical_not(has_right))
    def _():
        ex_v[QUAD : 3 * QUAD] = jnp.zeros((2 * QUAD, NF, 128), F32)
        xr[1] = jnp.zeros((8, 128), F32)
        pr[1] = jnp.zeros((ROWS, 128), F32)

    order = [(q, i) for pair in ((0, 2), (3, 1)) for i in range(0, QUAD, STEP) for q in pair]
    chunk = {}

    def send_chunks(which):
        for q, i in which:
            part = pl.ds(q * QUAD + i, STEP)
            chunk[q, i] = (to_right if q in (0, 3) else to_left)(e_v.at[part], ex_v.at[part])

    loads[0].wait()
    pl.semaphore_wait(barrier, 2 + has_left.astype(jnp.int32) + has_right.astype(jnp.int32))
    send_chunks(order[:AHEAD])

    rounds = (owners - 2 + 1) // 2

    def tell(r):
        if r < rounds:
            pl.semaphore_signal(word_sem.at[r, 0], inc=1, device_id=yp, device_id_type=MESH)
            pl.semaphore_signal(word_sem.at[r, 1], inc=1, device_id=ym, device_id_type=MESH)

    def hear(r):
        if r < rounds:
            pl.semaphore_wait(word_sem.at[r, 0], 1)
            pl.semaphore_wait(word_sem.at[r, 1], 1)
            tell(r + 1)

    tell(0)

    for cp in loads[1:5]:
        cp.wait()
    s_all, r_all = wide[0, 0:NF, :], wide[1, 0:NF, :]
    sums = []
    for q in range(4):

        def gather_energy(i, acc, q=q):
            d = q * QUAD + i
            e = e_v[d]
            return acc[0] + e, acc[1] + coef[d, 0] * e, acc[2] + coef[d, 1] * e

        zero = jnp.zeros((NF, 128), F32)
        sums.append(lax.fori_loop(0, QUAD, gather_energy, (zero, zero, zero), unroll=3))

    def over_f(x):
        return jnp.sum(x, axis=0, keepdims=True)

    gc = [x[1] for x in sums]
    gn = [x[2] for x in sums]
    en_xp, en_xm = over_f(s_all * (gc[0] + gc[3])), over_f(s_all * (gc[1] + gc[2]))
    en_yp, en_ym = over_f(s_all * (gn[0] + gn[1])), over_f(s_all * (gn[2] + gn[3]))
    en_own = over_f(sums[0][0] + sums[1][0] + sums[2][0] + sums[3][0]) - (en_xp + en_xm + en_yp + en_ym)
    en_yp, en_ym = pltpu.roll(en_yp, 1, 1), pltpu.roll(en_ym, 127, 1)

    w0, w1 = wind[0], wind[1]
    row8 = lax.broadcasted_iota(jnp.int32, (8, 128), 0)

    def tile(energy):
        return jnp.where(row8 == 0, energy, jnp.where(row8 == 1, w0, w1))

    xs[0], xs[1] = tile(en_xp), tile(en_xm)

    for side, last in ((0, 127), (1, 0)):
        pickup = jnp.where(lax.broadcasted_iota(jnp.int32, (16, 128), 1) == last, 1.0, 0.0).astype(BF16)
        high, low = split(flat_v[pl.ds(side * EDGE, EDGE), :])
        turned = (((1,), (1,)), ((), ()))
        ys[side, :, 0:128] = tile(en_yp if side == 0 else en_ym)
        ys[side, :, 128 : 128 + EDGE] = (mxu(pickup, high, turned) + mxu(pickup, low, turned))[0:8]
        ys[side, :, 128 + EDGE : 896] = jnp.zeros((8, 768 - EDGE), F32)
    early = [to_right(xs.at[0], xr.at[0]), to_left(xs.at[1], xr.at[1])]
    early += [to_up(ys.at[0], yr.at[0]), to_down(ys.at[1], yr.at[1])]

    send_chunks(order[AHEAD:])
    for cp in loads[5:]:
        cp.wait()

    hear(0)

    lane8 = lax.broadcasted_iota(jnp.int32, (1, owners), 1)
    point = lax.broadcasted_iota(jnp.int32, (128, 128), 0)
    slot = lax.rem(lane, CAP)
    for j in range(owners):
        to = lax.rem(o + j, owners)
        picked = rows[pl.ds(to, 1), :]
        number = jnp.sum(jnp.where(lane8 == to, count[...], 0).astype(F32), axis=1, keepdims=True).astype(jnp.int32)
        hit = jnp.concatenate([picked, picked], axis=1) == point
        at = pl.ds(j * 128, 128)
        all_slots[:, at] = jnp.where(hit, 1.0, 0.0).astype(BF16)
        live_slots[:, at] = jnp.where(jnp.logical_and(hit, slot < number), 1.0, 0.0).astype(BF16)

    hear(1)

    for j in range(owners):
        source = lax.rem(o + owners - j, owners)
        slots = lax.broadcasted_iota(jnp.int32, (CAP, opts), 0) + source * CAP
        total = jnp.zeros((CAP, opts), F32)
        for k in range(4):
            total = total + jnp.where(pick[k : k + 1, :] == slots, weight[k : k + 1, :], 0.0)
        high, low = split(total)
        m2[pl.ds(j * 128, CAP), :] = high
        m2[pl.ds(j * 128 + CAP, CAP), :] = low

    carried = current[...]
    ones = jnp.ones((1, opts), F32)
    c_high = carried.astype(BF16).astype(F32)
    none = jnp.zeros((5, opts), F32)
    car = jnp.concatenate([c_high, ones, none, carried - c_high, jnp.zeros((6, opts), F32)], axis=0).astype(BF16)
    t = mxu(car, m2[...], (((1,), (1,)), ((), ())))
    t = t[0:8] + t[8:16]
    for j in range(owners):
        part = t[:, j * 128 : j * 128 + 128]
        ts[j] = part + pltpu.roll(part, CAP, 1)
    for r in range(2, rounds):
        hear(r)
    returns = {j: send(ts.at[j], tr.at[j], peer(owners - j)) for j in far_first}

    for arrive, _ in early:
        arrive()
    ct, nt = wide[2, 0:NF, :], wide[3, 0:NF, :]

    def driving(a, b):
        return 0.1 * jnp.maximum(a * ct + b * nt, 0.0)

    drive[0] = driving(w0, w1)
    drive[1] = jnp.where(
        ct > 0, driving(xr[1, 1:2, :], xr[1, 2:3, :]), driving(xr[0, 1:2, :], xr[0, 2:3, :])
    )
    up0 = jnp.where(lane == 127, pltpu.roll(yr[1, 1:2, 0:128], 127, 1), pltpu.roll(w0, 127, 1))
    up1 = jnp.where(lane == 127, pltpu.roll(yr[1, 2:3, 0:128], 127, 1), pltpu.roll(w1, 127, 1))
    dn0 = jnp.where(lane == 0, pltpu.roll(yr[0, 1:2, 0:128], 1, 1), pltpu.roll(w0, 1, 1))
    dn1 = jnp.where(lane == 0, pltpu.roll(yr[0, 2:3, 0:128], 1, 1), pltpu.roll(w1, 1, 1))
    drive[2] = jnp.where(nt > 0, driving(up0, up1), driving(dn0, dn1))
    energy = (
        en_own
        + xr[0, 0:1, :]
        + xr[1, 0:1, :]
        + jnp.where(lane == 0, down_in * yr[0, 0:1, 0:128], en_yp)
        + jnp.where(lane == 127, up_in * yr[1, 0:1, 0:128], en_ym)
    ) * (1.0 / (ND * NF))
    damp = 0.3 * (energy / (energy + 1.0))

    for side, (last, inside, shift) in enumerate(((0, down_in, 1), (127, up_in, 127))):
        place = jnp.where(lax.broadcasted_iota(jnp.int32, (16, 128), 1) == last, 1.0, 0.0)
        place = jnp.where(lax.rem(lax.broadcasted_iota(jnp.int32, (16, 128), 0), 8) == 0, place, 0.0).astype(BF16)
        high, low = split(yr[side, :, 128 : 128 + EDGE] * inside)
        both = jnp.concatenate([high.astype(F32), low.astype(F32)], axis=0).astype(BF16)
        edge_v[side] = mxu(both, place, (((0,), (0,)), ((), ())))
        for half in (0, 1):
            for i in range(QUAD):
                d = side * 2 * QUAD + half * QUAD + i
                e = e_v[d]
                k = (half * QUAD + i) * NF
                behind = jnp.where(lane == last, edge_v[side, k : k + NF, :], pltpu.roll(e, shift, 1))
                m_v[d] = e + s_all * (coef[d, 1] * behind - coef[d, 8] * e)

    sea = mask[...].astype(F32)
    s_pad, r_pad = wide[0], wide[1]

    def contract(table, x):
        high, low = split(x)
        both = table[...].astype(BF16)
        out = mxu(both, high)
        return out[0:80] + out[80:160] + mxu(both[0:80], low)

    def finish(value, energy_row):
        tail = value[32:40] + jnp.where(row8 == 2, energy_row, 0.0)
        return (sea * jnp.concatenate([value[0:32], tail, value[40:80]], axis=0))[0:ROWS]

    def columns(acc_v, side):
        sums = [acc_v[side, g] for g in range(7)]
        parts = sums[1:5] + [sums[3] + r_pad * sums[5], sums[4] + r_pad * sums[6], jnp.zeros((16, 128), F32)]
        return jnp.concatenate(parts, axis=0), over_f(s_pad * sums[0])

    def advance(q, first):
        chunk[q, first][0]()
        x_side, y_side = (0 if q in (0, 3) else 1), (0 if q in (0, 1) else 1)
        for low, n in HALVES:
            part = pl.ds(low, n)
            r, s = wide[1, part, :], wide[0, part, :]
            acc = [ref[side, g, part, :] for ref, side in ((ax_v, x_side), (ay_v, y_side)) for g in range(7)]
            for i in range(STEP):
                d = q * QUAD + first + i
                moved = m_v[d, part, :] + s * (coef[d, 0] * ex_v[d, part, :])
                e = moved + moved * (r * (drive[0, d : d + 1, :] - damp))
                m_v[d, part, :] = e
                out = []
                for at, (a, kc, kn) in ((1, (0, 2, 3)), (2, (1, 4, 5))):
                    here = drive[at, d : d + 1, :]
                    e1 = e * here
                    e2 = e1 * here
                    a, kc, kn = coef[d, a], coef[d, kc], coef[d, kn]
                    out += [a * e, kc * e, kn * e, kc * e1, kn * e1, kc * e2, kn * e2]
                acc = [x + y for x, y in zip(acc, out)]
            for ref, side, values in ((ax_v, x_side, acc[:7]), (ay_v, y_side, acc[7:])):
                for g, value in enumerate(values):
                    ref[side, g, part, :] = value

    for q, first in order:
        if q in (0, 3):
            advance(q, first)
    sums_out = []

    def project(picks):
        sides = [columns(ref, side) for _, ref, side, _, _ in picks]
        out = contract(wxy, jnp.concatenate([x for x, _ in sides], axis=1))
        for i, (at, _, _, towards, shift) in enumerate(picks):
            value = finish(out[:, i * 128 : i * 128 + 128], sides[i][1])
            ps[at] = pltpu.roll(value, shift, 1) if shift else value
            sums_out.append(towards(ps.at[at], pr.at[at]))

    project([(0, ax_v, 0, to_right, 0)])
    for q, first in order:
        if q in (2, 1):
            advance(q, first)
    project([(2, ay_v, 0, to_up, 1), (3, ay_v, 1, to_down, 127), (1, ax_v, 1, to_left, 0)])

    e_own = []
    for low, n in HALVES:
        part = pl.ds(low, n)
        r, s = wide[1, part, :], wide[0, part, :]

        def own_bins(d, acc, part=part, s=s):
            e = m_v[d, part, :]
            e = e - s * (coef[d, 8] * e)
            here = drive[0, pl.ds(d, 1), :]
            e1 = e * here
            e2 = e1 * here
            kc, kn = coef[d, 6], coef[d, 7]
            out = (e, kc * e, kn * e, kc * e1, kn * e1, kc * e2, kn * e2)
            return tuple(x + y for x, y in zip(acc, out))

        a = lax.fori_loop(0, ND, own_bins, (jnp.zeros((n, 128), F32),) * 7, unroll=4)
        for g, value in enumerate([a[1], a[2], a[3], a[4], a[3] + r * a[5], a[4] + r * a[6]]):
            oq[pl.ds(g * FP + low, n), :] = value
        e_own.append(over_f(a[0]))
    total = finish(contract(wown, oq[...]), e_own[0] + e_own[1])

    for j in range(1, owners):
        returns[j][0]()
    sums = []
    for j in range(owners):
        value = tr[j] if j else ts[0]
        high = value.astype(BF16).astype(F32)
        sums.append(jnp.where(lane < CAP, high, value - high))
    sums = jnp.concatenate(sums, axis=1)
    sums = jnp.concatenate([sums, jnp.zeros(sums.shape, F32)], axis=0).astype(BF16)
    got = mxu(sums, all_slots[...], (((1,), (1,)), ((), ())))
    back[:, 0, :] = got[0:2] / jnp.maximum(got[2:3], 1.0)

    for arrive, _ in sums_out:
        arrive()
    total = (
        total
        + pr[0]
        + pr[1]
        + jnp.where(lane == 0, down_in * pr[2], ps[2])
        + jnp.where(lane == 127, up_in * pr[3], ps[3])
    )
    energy = total[34:35] * (1.0 / (ND * NF))
    value = sea * (total[0:CH] - (energy / (energy + 1.0)) * total[40:ROWS])

    half = CH // 2
    gap = jnp.zeros((24 - half, 128), F32)

    def two_parts(x):
        high = x.astype(BF16).astype(F32)
        return jnp.concatenate([high, x - high], axis=0).astype(BF16)

    out = mxu(two_parts(jnp.concatenate([value[0:half], gap, value[half:CH], gap], axis=0)), live_slots[...])
    out = out[0:48] + out[48:96]
    fields = {}
    for j in far_first + [0]:
        at = slice(j * 128, j * 128 + 128)
        fs[j] = jnp.where(lane < CAP, out[0:half, at], out[24 : 24 + half, at])
        if j:
            fields[j] = send(fs.at[j], fr.at[j], peer(j))

    acc = jnp.zeros((96, opts), F32)
    for j in range(0, owners, 2):
        sides = []
        for k in (j, j + 1):
            if k:
                fields[k][0]()
            value = jnp.concatenate([fr[k] if k else fs[0], gap], axis=0)
            other = pltpu.roll(value, CAP, 1)
            sides.append(two_parts(jnp.concatenate([jnp.where(lane < CAP, value, other), jnp.where(lane < CAP, other, value)], axis=0)))
        acc = acc + mxu(jnp.concatenate(sides, axis=1), m2[j * 128 : j * 128 + 256, :])
    acc = acc[0:48] + acc[48:96]
    forcing[0:half, :] = acc[0:half]
    forcing[half:CH, :] = acc[24 : 24 + half]

    for _, leave in (*early, *chunk.values(), *returns.values(), *sums_out, *fields.values()):
        leave()


def write_out(forcing, back, forcing_hbm, back_hbm, sem):
    copies = [pltpu.make_async_copy(forcing, forcing_hbm, sem.at[0]), pltpu.make_async_copy(back, back_hbm, sem.at[1])]
    for cp in copies:
        cp.start()
    for cp in copies:
        cp.wait()


def per_device(spectra, surface_wind, water_mask, send_rows, send_count, pick_slot, pick_weight, ocean_current):
    strips, owners = lax.axis_size("wave"), lax.axis_size("ocean")
    opts = pick_slot.shape[1]
    coef, wide, wown, wxy = (jnp.asarray(x) for x in constants())
    anywhere = pl.BlockSpec(memory_space=pltpu.HBM)
    copies = 8 + ND // STEP + 2 * (owners - 1)

    def f32(*shape):
        return pltpu.VMEM(shape, F32)

    def i32(*shape):
        return pltpu.VMEM(shape, jnp.int32)

    results = pl.pallas_call(
        functools.partial(interval, strips, owners, opts),
        name="interval",
        out_shape=(
            jax.ShapeDtypeStruct((34, opts), F32),
            jax.ShapeDtypeStruct((2, 1, 128), F32),
        ),
        in_specs=[anywhere] * 13,
        out_specs=(pl.BlockSpec(memory_space=pltpu.VMEM),) * 2,
        scratch_shapes=[
            pltpu.SMEM((ND, 16), F32),
            f32(ND, NF, 128),
            f32(ND, NF, 128),
            f32(ND, NF, 128),
            f32(ND * NF, 128),
            f32(2, EDGE, 128),
            f32(2, 1, 128),
            i32(1, 128),
            i32(owners, CAP),
            i32(1, owners),
            i32(4, opts),
            f32(4, opts),
            f32(2, opts),
            f32(4, FP, 128),
            f32(160, 256),
            f32(160, 256),
            f32(3, NF, 128),
            f32(2, 7, FP, 128),
            f32(2, 7, FP, 128),
            f32(256, 128),
            f32(2, 8, 128),
            f32(2, 8, 128),
            f32(2, 8, 896),
            f32(2, 8, 896),
            f32(4, ROWS, 128),
            f32(4, ROWS, 128),
            f32(owners, CH // 2, 128),
            f32(owners, CH // 2, 128),
            f32(owners, 8, 128),
            f32(owners, 8, 128),
            pltpu.VMEM((owners * 128, opts), BF16),
            pltpu.VMEM((128, owners * 128), BF16),
            pltpu.VMEM((128, owners * 128), BF16),
            pltpu.SemaphoreType.DMA((13,)),
            pltpu.SemaphoreType.DMA((copies,)),
            pltpu.SemaphoreType.DMA((copies,)),
            pltpu.SemaphoreType.REGULAR((max((owners - 1) // 2, 1), 2)),
        ],
        compiler_params=pltpu.CompilerParams(collective_id=0, has_side_effects=True, vmem_limit_bytes=32 << 20),
    )(
        *(
            pltpu.with_memory_space_constraint(x, pltpu.HBM)
            for x in (
                coef,
                spectra.reshape(ND, NF, 1, 128),
                spectra.reshape(ND * NF, 128),
                surface_wind,
                water_mask,
                send_rows,
                send_count.reshape(1, owners),
                pick_slot,
                pick_weight,
                ocean_current,
                wide,
                wown,
                wxy,
            )
        )
    )
    return pl.pallas_call(
        write_out,
        name="write_out",
        out_shape=(
            jax.ShapeDtypeStruct((34, opts), F32),
            jax.ShapeDtypeStruct((2, 1, 128), F32),
        ),
        in_specs=[pl.BlockSpec(memory_space=pltpu.VMEM)] * 2,
        out_specs=(anywhere,) * 2,
        scratch_shapes=[pltpu.SemaphoreType.DMA((2,))],
    )(*(pltpu.with_memory_space_constraint(x, pltpu.VMEM) for x in results))


def solution(mesh):
    in_specs = (
        P("wave", None, None, "ocean"),
        P(None, "wave", "ocean"),
        P("wave", "ocean"),
        P(None, ("wave", "ocean")),
        P(None, ("wave", "ocean")),
        P(None, ("wave", "ocean")),
        P(None, ("wave", "ocean")),
        P(None, ("wave", "ocean")),
    )
    out_specs = (P(None, ("wave", "ocean")), P(None, "wave", "ocean"))
    return jax.shard_map(per_device, mesh=mesh, in_specs=in_specs, out_specs=out_specs, check_vma=False)
```
